512 devices in a mesh: dp: 32 (over y, x_lo, core), seq: 16 (over z, x_hi).
Axes of the slice: x: 4 (x_hi: 2, x_lo: 2; x = x_hi * 2 + x_lo), y: 8, z: 8, core: 2. Of those that a mesh axis runs over, the one named last changes fastest.
Arguments:
- tokens: int32 [32, 4096], P('dp', 'seq'), may hold values from 0 to 3
- embedding: float32 [4, 384], replicated, may hold values from -6 to 6
- gain_in: float32 [384], replicated, may hold values from 0.5 to 1.5
- conv_taps: float32 [384, 4], replicated, may hold values from -3 to 3
- long_filter: float32 [384, 1024], P('seq'), may hold values from -6 to 6
- gain_mid: float32 [384], replicated, may hold values from 0.5 to 1.5
- mlp_weights: bfloat16 [2304, 384], replicated, may hold values from -0.3125 to 0.3125
- cotangent: bfloat16 [32, 768, 4096], P('dp', None, 'seq'), may hold values from -6 to 6
Outputs:
- layer_out: bfloat16 [32, 768, 4096], P('dp', None, 'seq')
- grad_embedding: float32 [4, 384], replicated
- grad_gain_in: float32 [384], replicated
- grad_conv: float32 [384, 4], replicated
- grad_filter: float32 [384, 1024], P('seq')
- grad_gain_mid: float32 [384], replicated
- grad_mlp: float32 [2304, 384], P('dp', 'seq')
The draws below stay inside these ranges and needn't reach their ends.
All inputs are finite; a program needn't handle non-finite values.
Results may differ from the reference program's by a relative error of at most 0.03.
Values may be sent and summed in bfloat16 or wider, within the bound.
No kernel may reach another device: no remote copies, remote signals or barrier semaphores. Data moves between devices by JAX's collectives and lax.ppermute only.
A program may use at most 64 MiB of HBM per device.

```python
from functools import partial
import jax
import jax.numpy as jnp
from jax import lax

D = 384
FF = 768
GROUP = 1024
KW = 4
LEN = 4096
BATCH = 32


def plant(values, key, least, top_value):
    extent = values.shape
    spot = [jax.random.randint(jax.random.fold_in(key, axis), (), 0, extent[axis]) for axis in range(len(extent))]
    values = values.at[tuple(spot)].set(least)
    longest = extent.index(max(extent))
    spot[longest] = (spot[longest] + 1) % extent[longest]
    return values.at[tuple(spot)].set(top_value)


def steps_of(own_key, shape, shards, least, high):
    loudness, own = 1.0, jax.random.fold_in(own_key, 6)
    for axis_at, shards_of in shards:
        draws = jnp.exp(jax.random.uniform(jax.random.fold_in(own, axis_at), (shards_of,), jnp.float32, least / len(shards), high / len(shards)))
        loudness = loudness * jnp.repeat(draws, shape[axis_at] // shards_of).reshape([-1 if axis == axis_at else 1 for axis in range(len(shape))])
    return loudness


def bell_draw(stream_key, shape, spread, reach, cuts=(), kind=jnp.bfloat16):
    values = spread * jax.random.normal(stream_key, shape, jnp.float32)
    if cuts:
        values = values * steps_of(stream_key, shape, cuts, -0.22, 0.18)
    return jnp.clip(values, -reach, reach).astype(kind)


def setup_inputs(seed: int = 0) -> dict:
    streams_of = jax.random.split(jax.random.key(seed), 9)
    tokens = plant(jax.random.randint(streams_of[0], (BATCH, LEN), 0, 4), jax.random.fold_in(streams_of[0], 1), 0, 3).astype(jnp.int32)
    embedding = bell_draw(streams_of[1], (4, D), 1.0, 6.0, (), jnp.float32)
    gain_in = jnp.clip(1.0 + 0.1 * jax.random.normal(streams_of[2], (D,), jnp.float32), 0.5, 1.5)
    conv_taps = bell_draw(streams_of[3], (D, KW), KW ** -0.5, 3.0, (), jnp.float32)
    long_filter = bell_draw(streams_of[4], (D, GROUP), 1.0, 6.0, ((0, 16),), jnp.float32)
    gain_mid = jnp.clip(1.0 + 0.1 * jax.random.normal(streams_of[5], (D,), jnp.float32), 0.5, 1.5)
    mlp_weights = bell_draw(streams_of[6], (3 * FF, D), D ** -0.5, 0.3125)
    cotangent = bell_draw(streams_of[7], (BATCH, 2 * D, LEN), 1.0, 6.0, ((0, 32), (2, 16)))
    return dict(tokens=tokens, embedding=embedding, gain_in=gain_in, conv_taps=conv_taps, long_filter=long_filter, gain_mid=gain_mid, mlp_weights=mlp_weights, cotangent=cotangent)


def dct_table(length):
    freq = jnp.arange(length, dtype=jnp.int32)[:, None]
    place = jnp.arange(length, dtype=jnp.int32)[None, :]
    phase = (2 * place + 1) * freq % (4 * length)
    weight = jnp.where(freq == 0, jnp.sqrt(1.0 / length), jnp.sqrt(2.0 / length))
    angle = jnp.pi * phase.astype(jnp.float32) / (2 * length)
    return (weight * jnp.cos(angle)).astype(jnp.bfloat16)

def rms_gain(values, gain):
    scale = lax.rsqrt(lax.optimization_barrier(jnp.mean(values * values, axis=-2, keepdims=True)) + 1e-06)
    return (values * scale * gain[:, None]).astype(jnp.bfloat16)

def lookup_norm(embedding, gain_in, onehot):
    residual = jnp.einsum('kd,sbkl->sbdl', embedding, onehot, precision=lax.Precision.HIGHEST)
    return (residual, rms_gain(residual, gain_in))

def conv_before(padded, conv_taps):
    rim_width = conv_taps.shape[1] - 1
    length = padded.shape[-1] - rim_width
    summed = conv_taps[:, 0][:, None] * padded[..., rim_width:rim_width + length]
    for tap_index in range(1, rim_width + 1):
        start = rim_width - tap_index
        summed = summed + conv_taps[:, tap_index][:, None] * padded[..., start:start + length]
    return summed.astype(jnp.bfloat16)

def group_filter(mixed, long_filter, dct_rows):
    strands, batch, channels, length = mixed.shape
    block_len = dct_rows.shape[0]
    blocks = mixed.astype(jnp.float32).reshape(strands, batch, channels, length // block_len, block_len)
    table_f = dct_rows.astype(jnp.float32)
    spectrum = jnp.einsum('sbdni,ki->sbdnk', blocks, table_f, precision=lax.Precision.HIGHEST).astype(jnp.bfloat16)
    scaled = (long_filter[None, None, :, None, :] * spectrum.astype(jnp.float32)).astype(jnp.bfloat16)
    restored = jnp.einsum('sbdnk,ki->sbdni', scaled.astype(jnp.float32), table_f, precision=lax.Precision.HIGHEST)
    return restored.astype(jnp.bfloat16).reshape(strands, batch, channels, length)

def mid_norm(residual, filtered, gain_mid):
    level = residual + filtered.astype(jnp.float32)
    return (level, rms_gain(level, gain_mid))

def feed_forward(level, normed_mid, weights):
    projected = jnp.einsum('fd,sbdl->sbfl', weights[:2 * FF], normed_mid.astype(jnp.float32), precision=lax.Precision.HIGHEST).astype(jnp.bfloat16)
    both_parts = projected.astype(jnp.float32)
    gate_in = both_parts[:, :, :FF]
    up_value = both_parts[:, :, FF:]
    activated = (jax.nn.silu(gate_in) * up_value).astype(jnp.bfloat16)
    down = jnp.einsum('fd,sbfl->sbdl', weights[2 * FF:], activated.astype(jnp.float32), precision=lax.Precision.HIGHEST)
    return (level + down).astype(jnp.bfloat16)

def strand_layer(base_ids, dct_rows, embedding, gain_in, conv_taps, long_filter, gain_mid, weights):
    strands = jnp.stack([base_ids, 3 - jnp.flip(base_ids, 0)])[:, None, :]
    onehot = (strands[:, :, None, :] == jnp.arange(4, dtype=jnp.int32)[None, None, :, None]).astype(jnp.float32)
    residual, normed = lookup_norm(embedding, gain_in, onehot)
    padded = jnp.pad(normed.astype(jnp.float32), ((0, 0), (0, 0), (0, 0), (KW - 1, 0)))
    mixed = conv_before(padded, conv_taps)
    filtered = group_filter(mixed, long_filter, dct_rows)
    level, normed_mid = mid_norm(residual, filtered, gain_mid)
    result = feed_forward(level, normed_mid, weights)
    return jnp.concatenate([result[0, 0], jnp.flip(result[1, 0], (0, 1))], 0)

def reference(tokens, embedding, gain_in, conv_taps, long_filter, gain_mid, mlp_weights, cotangent):
    dct_rows = dct_table(GROUP)
    params = (embedding, gain_in, conv_taps, long_filter, gain_mid, mlp_weights.astype(jnp.float32))

    def one_sequence(running, sliced):
        base_ids, seq_cot = sliced
        layer_part, pullback = jax.vjp(partial(strand_layer, base_ids, dct_rows), *params)
        gradients = pullback(seq_cot)
        return (tuple((summed_grad + fresh_grad for summed_grad, fresh_grad in zip(running, gradients))), layer_part)
    zeros = tuple((jnp.zeros(param.shape, jnp.float32) for param in params))
    totals, layer_out = lax.scan(one_sequence, zeros, (tokens, cotangent))
    return (layer_out, totals[0], totals[1], totals[2], totals[3], totals[4], totals[5])
```

```python
from functools import partial

import jax
import jax.numpy as jnp
import numpy as np
from jax import lax
from jax.experimental import pallas as pl
from jax.experimental.pallas import tpu as pltpu
from jax.sharding import Mesh
from jax.sharding import PartitionSpec as P

DP = ("dp_y", "dp_x", "dp_c")
CHIPS = ("dp_y", "dp_x")
SEQ = ("seq_z", "seq_x")
F32, BF16 = jnp.float32, jnp.bfloat16
LANES = 128


def dct_table(length):
    freq = np.arange(length, dtype=np.int64)[:, None]
    place = np.arange(length, dtype=np.int64)[None, :]
    phase = (2 * place + 1) * freq % (4 * length)
    weight = np.where(freq == 0, np.sqrt(1.0 / length), np.sqrt(2.0 / length))
    return (weight * np.cos(np.pi * phase / (2 * length))).astype(np.float32).astype(jnp.bfloat16)


def dot(a, b):
    return jnp.dot(a, b, preferred_element_type=F32)


def dot_nt(a, b):
    return lax.dot_general(a, b, (((1,), (1,)), ((), ())), preferred_element_type=F32)


def layer_kernel(
    where_ref, gath, tok_ref, cols, acat, w, wt, qt, qown, cot,
    out, keep, send, red,
    lf_s, spec_s, scaled_s, m_s, act_s, bproj_s, bo_s, df_s, gf_s, acc_s,
):
    shards = gath.shape[0]
    dim, group = lf_s.shape
    own_ch = dim // shards
    hidden = act_s.shape[0]
    span = tok_ref.shape[1]
    chunks = group // LANES
    body_rows = chunks * own_ch
    per_block = group // span
    place = where_ref[0]
    core = where_ref[1]
    block = place // per_block
    first = block * per_block
    inner = place - first

    for sh in range(shards):
        x = gath[sh, 0:body_rows, :].astype(F32)
        for c in range(chunks):
            lf_s[sh * own_ch : (sh + 1) * own_ch, c * LANES : (c + 1) * LANES] = x[
                c * own_ch : (c + 1) * own_ch, :
            ]

    rows_of = span // LANES
    tail = gath.shape[1] - 16

    def ids_of(shard):
        return gath[shard, tail : tail + 16, :].astype(F32)

    before = ids_of(jnp.maximum(first - 1, 0))[rows_of - 1 : rows_of, :]
    before = jnp.where(block > 0, before, -1.0)
    last = first + per_block
    after = ids_of(jnp.minimum(last, shards - 1))[0:1, :]
    after = jnp.where(last < shards, after, -1.0)
    pieces = [before]
    for q in range(per_block):
        ids = ids_of(first + q)
        pieces += [ids[j : j + 1, :] for j in range(rows_of)]
    pieces.append(after)
    ext = jnp.concatenate([jnp.broadcast_to(p, (8, LANES)) for p in pieces], axis=1)
    width = group + 2 * LANES
    row = lax.broadcasted_iota(jnp.int32, (32, group), 0)
    picked = jnp.zeros((32, group), F32)
    for j in range(8):
        shift = j if j < 4 else (width - (j - 4)) % width
        moved = ext if shift == 0 else pltpu.roll(ext, shift, 1)
        moved = jnp.broadcast_to(moved[0:1, LANES : LANES + group], (32, group))
        picked = jnp.where(row // 4 == j, moved, picked)
    want = jnp.where(row < 16, row % 4, 3 - row % 4).astype(F32)
    onehot = jnp.where(picked == want, 1.0, 0.0).astype(BF16)
    ohq = dot(onehot, qt[...])
    high = ohq.astype(BF16)
    low = (ohq - high.astype(F32)).astype(BF16)

    emb = cols[:, 0:4]
    taps = cols[:, 4:8]
    ntab = cols[:, 8:12]
    gin = cols[:, 12:13]
    gmid = cols[:, 13:14]
    tok = tok_ref[...].astype(F32)
    ri = lax.broadcasted_iota(jnp.int32, (dim, dim), 0)
    ci = lax.broadcasted_iota(jnp.int32, (dim, dim), 1)
    turn = jnp.where(ri + ci == dim - 1, 1.0, 0.0).astype(BF16)
    bo_s[:, 0:span] = cot[0:dim, :]
    bo_s[:, span : 2 * span] = dot(turn, cot[dim : 2 * dim, :]).astype(BF16)

    step = 128
    gmid_part = jnp.zeros((dim, 1), F32)
    direct = jnp.zeros((dim, 16), F32)
    taps_part = [jnp.zeros((step, 16), F32) for _ in range(dim // step)]
    own_q = qt.at[pl.ds(pl.multiple_of(inner * span, span), span), :]
    for s in range(2):
        here = slice(s * span, (s + 1) * span)
        o_high = high[16 * s : 16 * s + 16]
        o_low = low[16 * s : 16 * s + 16]
        ocat = jnp.concatenate([o_high, o_high, o_low], axis=0)
        opair = jnp.concatenate([o_high, o_low], axis=0)
        for r in range(0, dim, step):
            spec = dot(acat[r : r + step, :], ocat).astype(BF16)
            spec_s[s, r : r + step, :] = spec
            scaled_s[r : r + step, :] = (lf_s[r : r + step, :] * spec.astype(F32)).astype(BF16)
        filt = dot(scaled_s[...], qown[...]).astype(BF16).astype(F32)
        ids = tok if s == 0 else 3.0 - tok
        resid = jnp.broadcast_to(emb[:, 3:4], (dim, span))
        for t in range(3):
            resid = jnp.where(ids == float(t), emb[:, t : t + 1], resid)
        level = resid + filt
        scale = lax.rsqrt(jnp.sum(level * level, axis=0, keepdims=True) * (1.0 / dim) + 1e-06)
        m_s[:, here] = (level * scale * gmid).astype(BF16)
        normed = m_s[:, here]
        back = bo_s[:, here]
        part = 256
        for h in range(0, hidden, part):
            gate = dot(w[h : h + part, :], normed).astype(BF16).astype(F32)
            up = dot(w[hidden + h : hidden + h + part, :], normed).astype(BF16).astype(F32)
            ba = dot(w[2 * hidden + h : 2 * hidden + h + part, :], back).astype(BF16).astype(F32)
            sig = jax.nn.sigmoid(gate)
            swish = gate * sig
            act_s[h : h + part, here] = (swish * up).astype(BF16)
            bproj_s[h : h + part, here] = (ba * up * sig * (1.0 + gate * (1.0 - sig))).astype(BF16)
            bproj_s[hidden + h : hidden + h + part, here] = (ba * swish).astype(BF16)
        z = (level + dot(wt[:, 2 * hidden : 3 * hidden], act_s[:, here])).astype(BF16)
        if s == 0:
            out[0:dim, :] = z
        else:
            out[dim : 2 * dim, :] = dot(turn, z).astype(BF16)
        bmid = dot(wt[:, 0 : 2 * hidden], bproj_s[:, here]).astype(BF16).astype(F32)
        gmid_part += jnp.sum(bmid * level * scale, axis=1, keepdims=True)
        weighed = bmid * gmid
        pull = jnp.sum(weighed * level, axis=0, keepdims=True)
        dlevel = (
            back.astype(F32) + scale * weighed - level * (scale * scale * scale * pull * (1.0 / dim))
        )
        dfilt = dlevel.astype(BF16)
        df_s[...] = dfilt
        base = lax.broadcasted_iota(jnp.int32, (16, span), 0).astype(F32)
        mine = jnp.where(ids == base, 1.0, 0.0).astype(BF16)
        direct += dot_nt(dfilt, mine)
        for i, r in enumerate(range(0, dim, step)):
            ds = dot(df_s[r : r + step, :], own_q[...])
            term = ds * spec_s[s, r : r + step, :].astype(F32)
            if s == 0:
                gf_s[r : r + step, :] = term
            else:
                gf_s[r : r + step, :] += term
            dspec = (lf_s[r : r + step, :] * ds).astype(BF16)
            both = dot_nt(dspec, opair)
            taps_part[i] += both[:, 0:16] + both[:, 16:32]

    g = jnp.concatenate(taps_part, axis=0)
    dn = jnp.zeros((dim, 4), F32)
    conv = []
    for k in range(4):
        gk = g[:, 4 * k : 4 * k + 4]
        dn += taps[:, k : k + 1] * gk
        conv.append(jnp.sum(ntab * gk, axis=1, keepdims=True))
    escale = lax.rsqrt(jnp.sum(emb * emb, axis=0, keepdims=True) * (1.0 / dim) + 1e-06)
    epull = jnp.sum(gin * dn * emb, axis=0, keepdims=True)
    demb = escale * gin * dn - emb * (escale * escale * escale * epull * (1.0 / dim))
    demb += direct[:, 0:4]
    dgin = jnp.sum(dn * emb * escale, axis=1, keepdims=True)
    lane = lax.broadcasted_iota(jnp.int32, (dim, LANES), 1)
    small = jnp.zeros((dim, LANES), F32)
    values = [demb[:, t : t + 1] for t in range(4)] + [dgin] + conv + [gmid_part]
    for i, val in enumerate(values):
        small = jnp.where(lane == i, val, small)
    fill = jnp.zeros((red.shape[1] - body_rows - own_ch, LANES), F32)
    for sh in range(shards):
        rows = slice(sh * own_ch, (sh + 1) * own_ch)
        tiles = [gf_s[rows, c * LANES : (c + 1) * LANES] for c in range(chunks)]
        red[sh] = jnp.concatenate(tiles + [small[rows, :], fill], axis=0).astype(BF16)

    for r in range(0, 2 * hidden, 256):
        acc_s[r : r + 256, :] = dot_nt(bproj_s[r : r + 256, :], m_s[...])
    for r in range(0, hidden, 256):
        acc_s[2 * hidden + r : 2 * hidden + r + 256, :] = dot_nt(act_s[r : r + 256, :], bo_s[...])
    chips, rows, _ = keep.shape
    pair = acc_s.shape[0] // chips
    for i in range(chips):
        keep[i] = acc_s[pl.ds(pl.multiple_of(i * pair + core * rows, 8), rows), :].astype(BF16)
        if pair > rows:
            other = i * pair + (1 - core) * rows
            send[i] = acc_s[pl.ds(pl.multiple_of(other, 8), rows), :].astype(BF16)


def to_all(x, axis):
    size = lax.axis_size(axis)
    return lax.all_to_all(jnp.broadcast_to(x[None], (size, *x.shape)), axis, 0, 0, tiled=True)


def split_to(x, axis):
    return lax.all_to_all(x, axis, 0, 0, tiled=True)


def on_device(tokens, embedding, gain_in, conv_taps, long_filter, gain_mid, mlp_weights, cotangent):
    span = tokens.shape[1]
    dim = embedding.shape[1]
    hidden = mlp_weights.shape[0] // 3
    own_ch, group = long_filter.shape
    shards = lax.axis_size(SEQ)
    dps = lax.axis_size(DP)
    chips = lax.axis_size(CHIPS)
    cores = dps // chips
    chunks = group // LANES
    body_rows = chunks * own_ch
    place = lax.axis_index(SEQ)
    core = lax.axis_index("dp_c")

    body = jnp.swapaxes(long_filter.astype(BF16).reshape(own_ch, chunks, LANES), 0, 1)
    ids = tokens.astype(BF16).reshape(span // LANES, LANES)
    msg = jnp.concatenate([body.reshape(body_rows, LANES), jnp.pad(ids, ((0, 16 - span // LANES), (0, 0)))])
    gath = to_all(msg, SEQ)

    table = dct_table(group)
    qt = jnp.asarray(np.ascontiguousarray(table.T))
    qown = lax.dynamic_slice_in_dim(jnp.asarray(table), (place % (group // span)) * span, span, 1)
    emb_t = embedding.T
    escale = lax.rsqrt(jnp.mean(emb_t * emb_t, axis=0, keepdims=True) + 1e-06)
    ntab = (emb_t * escale * gain_in[:, None]).astype(BF16).astype(F32)
    coef = (conv_taps[:, :, None] * ntab[:, None, :]).reshape(dim, 16)
    chigh = coef.astype(BF16)
    clow = (coef - chigh.astype(F32)).astype(BF16)
    acat = jnp.concatenate([chigh, clow, chigh], axis=1)
    cols = jnp.concatenate(
        [emb_t, conv_taps, ntab, gain_in[:, None], gain_mid[:, None], jnp.zeros((dim, 2), F32)], axis=1
    )
    where = jnp.stack([place, core]).astype(jnp.int32)
    wt = mlp_weights.T

    own_rows = 3 * hidden // dps
    red_rows = body_rows + own_ch
    red_rows += -red_rows % 16
    vmem = pl.BlockSpec(memory_space=pltpu.VMEM)
    layer, keep, send, red = pl.pallas_call(
        layer_kernel,
        out_shape=(
            jax.ShapeDtypeStruct((2 * dim, span), BF16),
            jax.ShapeDtypeStruct((chips, own_rows, dim), BF16),
            jax.ShapeDtypeStruct((chips, own_rows, dim), BF16),
            jax.ShapeDtypeStruct((shards, red_rows, LANES), BF16),
        ),
        in_specs=[pl.BlockSpec(memory_space=pltpu.SMEM)] + [vmem] * 9,
        out_specs=[vmem] * 4,
        scratch_shapes=[
            pltpu.VMEM((dim, group), F32),
            pltpu.VMEM((2, dim, group), BF16),
            pltpu.VMEM((dim, group), BF16),
            pltpu.VMEM((dim, 2 * span), BF16),
            pltpu.VMEM((hidden, 2 * span), BF16),
            pltpu.VMEM((2 * hidden, 2 * span), BF16),
            pltpu.VMEM((dim, 2 * span), BF16),
            pltpu.VMEM((dim, span), BF16),
            pltpu.VMEM((dim, group), F32),
            pltpu.VMEM((3 * hidden, dim), F32),
        ],
        compiler_params=pltpu.CompilerParams(vmem_limit_bytes=52 * 1024 * 1024),
        name="layer",
    )(where, gath, tokens, cols, acat, mlp_weights, wt, qt, qown, cotangent[0])

    parts = split_to(red, SEQ).astype(F32).sum(0)
    if cores > 1:
        came = lax.ppermute(send, "dp_c", [(0, 1), (1, 0)])
        keep = (keep.astype(F32) + came.astype(F32)).astype(BF16)
    row_block = split_to(keep, CHIPS).astype(F32).sum(0)

    small_n = 10
    small = parts[body_rows : body_rows + own_ch, :small_n].T.reshape(1, small_n * own_ch)
    piece = body_rows * LANES // dps
    lanes = piece + small_n * own_ch
    lanes += -lanes % 256
    packed = jnp.concatenate(
        [
            parts[:body_rows].reshape(dps, piece),
            jnp.broadcast_to(small, (dps, small_n * own_ch)),
            jnp.zeros((dps, lanes - piece - small_n * own_ch), F32),
        ],
        axis=1,
    ).astype(BF16)
    summed = split_to(packed.reshape(dps, lanes // LANES, LANES), DP).astype(F32).sum(0).reshape(lanes)
    whole = to_all(summed[:piece].astype(BF16).reshape(piece // LANES, LANES), DP)
    grad_filter = (
        jnp.swapaxes(whole.astype(F32).reshape(chunks, own_ch, LANES), 0, 1).reshape(own_ch, group)
    )
    everyone = to_all(summed[piece : piece + small_n * own_ch].reshape(small_n, own_ch), SEQ)
    everyone = jnp.swapaxes(everyone, 0, 1).reshape(small_n, dim)
    grad_embedding = everyone[0:4]
    grad_gain_in = everyone[4]
    grad_conv = everyone[5:9].T
    grad_gain_mid = everyone[9]
    blocks = jnp.swapaxes(row_block.reshape(own_rows, shards, dim // shards), 0, 1)
    grad_mlp = split_to(blocks, SEQ).sum(0)
    return layer[None], grad_embedding, grad_gain_in, grad_conv, grad_filter, grad_gain_mid, grad_mlp


def solution(mesh):
    dps, seqs = mesh.devices.shape
    cores = 2 if dps > 1 else 1
    across = 2 if dps > 2 else 1
    torus = Mesh(
        mesh.devices.reshape(dps // (across * cores), across, cores, seqs // 2, 2), DP + SEQ
    )
    return jax.shard_map(
        on_device,
        mesh=torus,
        in_specs=(P(DP, SEQ), P(), P(), P(), P(SEQ, None), P(), P(), P(DP, None, SEQ)),
        out_specs=(P(DP, None, SEQ), P(), P(), P(), P(SEQ, None), P(), P(DP, SEQ)),
        check_vma=False,
    )
```

```python
from functools import partial

import jax
import jax.numpy as jnp
import numpy as np
from jax import lax
from jax.experimental import pallas as pl
from jax.experimental.pallas import tpu as pltpu
from jax.sharding import Mesh
from jax.sharding import PartitionSpec as P

DP = ("dp_y", "dp_x", "dp_c")
SEQ = ("seq_z", "seq_x")
F32, BF16 = jnp.float32, jnp.bfloat16
LANES = 128


def dct_table(length):
    freq = np.arange(length, dtype=np.int64)[:, None]
    place = np.arange(length, dtype=np.int64)[None, :]
    phase = (2 * place + 1) * freq % (4 * length)
    weight = np.where(freq == 0, np.sqrt(1.0 / length), np.sqrt(2.0 / length))
    return (weight * np.cos(np.pi * phase / (2 * length))).astype(np.float32).astype(jnp.bfloat16)


def dot(a, b):
    return jnp.dot(a, b, preferred_element_type=F32)


def dot_nt(a, b):
    return lax.dot_general(a, b, (((1,), (1,)), ((), ())), preferred_element_type=F32)


def onehot_rows(gath, groups, group, half_rows, per_block):
    shards = gath.shape[0]
    rows_of = 2
    ids = [gath[sh, half_rows : half_rows + 16, :].astype(F32) for sh in range(shards)]
    rows = [ids[sh][j : j + 1, :] for sh in range(shards) for j in range(rows_of)]
    outside = jnp.full((1, LANES), -1.0, F32)
    rows = [outside] + rows + [outside]
    per = per_block * rows_of
    width = group + 2 * LANES
    row = lax.broadcasted_iota(jnp.int32, (32, group), 0)
    want = jnp.where(row < 16, row % 4, 3 - row % 4).astype(F32)
    onehots = []
    for b in range(groups):
        pieces = rows[b * per : b * per + per + 2]
        ext = jnp.concatenate([jnp.broadcast_to(p, (8, LANES)) for p in pieces], axis=1)
        picked = jnp.zeros((32, group), F32)
        for j in range(8):
            shift = j if j < 4 else (width - (j - 4)) % width
            moved = ext if shift == 0 else pltpu.roll(ext, shift, 1)
            moved = jnp.broadcast_to(moved[0:1, LANES : LANES + group], (32, group))
            picked = jnp.where(row // 4 == j, moved, picked)
        onehots.append(jnp.where(picked == want, 1.0, 0.0).astype(BF16))
    return onehots


def dct_kernel(gath, acat, qt, ohq, spec, *, half_rows, per_block):
    own_ch = acat.shape[0]
    _, groups, _, group = ohq.shape
    onehots = onehot_rows(gath, groups, group, half_rows, per_block)
    both = dot(jnp.concatenate(onehots, axis=0), qt[...])
    for b in range(groups):
        x = both[32 * b : 32 * b + 32, :]
        high = x.astype(BF16)
        low = (x - high.astype(F32)).astype(BF16)
        for s in range(2):
            o_high = high[16 * s : 16 * s + 16]
            o_low = low[16 * s : 16 * s + 16]
            ocat = jnp.concatenate([o_high, o_high, o_low], axis=0)
            ohq[s, b] = ocat
            at = (s * groups + b) * own_ch
            spec[at : at + own_ch, :] = dot(acat[...], ocat)


def back_kernel(cot, w_down, bo, ba):
    dim, span = cot.shape[0] // 2, cot.shape[1]
    ri = lax.broadcasted_iota(jnp.int32, (dim, dim), 0)
    ci = lax.broadcasted_iota(jnp.int32, (dim, dim), 1)
    turn = jnp.where(ri + ci == dim - 1, 1.0, 0.0).astype(BF16)
    bo[:, 0:span] = cot[0:dim, :]
    bo[:, span : 2 * span] = dot(turn, cot[dim : 2 * dim, :]).astype(BF16)
    for r in range(0, w_down.shape[0], 256):
        ba[r : r + 256, :] = dot(w_down[r : r + 256, :], bo[...]).astype(BF16)


def mid_kernel(
    where_ref, ga, gb, tok_ref, cols, acat, w, wt, qown, ohq, bo, ba,
    msg, m_s, act_s, bproj_s, level_s,
    lf_s, scaled_s, df_s,
):
    shards = ga.shape[0]
    chunks, dim, _ = lf_s.shape
    own_ch = dim // shards
    hidden = act_s.shape[0]
    span = tok_ref.shape[1]
    half = chunks // 2
    body_rows = half * own_ch
    core = where_ref[1]
    block = where_ref[2]
    for sh in range(shards):
        for c in range(half):
            rows = slice(c * own_ch, (c + 1) * own_ch)
            dst = slice(sh * own_ch, (sh + 1) * own_ch)
            lf_s[core * half + c, dst, :] = ga[sh, 0:body_rows, :].astype(F32)[rows, :]
            lf_s[(1 - core) * half + c, dst, :] = gb[sh, 0:body_rows, :].astype(F32)[rows, :]
    emb = cols[:, 0:4]
    gmid = cols[:, 13:14]
    tok = tok_ref[...].astype(F32)
    step = 128
    gmid_part = jnp.zeros((dim, 1), F32)
    direct = jnp.zeros((dim, 16), F32)
    for s in range(2):
        here = slice(s * span, (s + 1) * span)
        ocat = ohq[s, block]
        for r in range(0, dim, step):
            spec = dot(acat[r : r + step, :], ocat).astype(BF16).astype(F32)
            for c in range(chunks):
                lanes = slice(c * LANES, (c + 1) * LANES)
                scaled_s[r : r + step, lanes] = (lf_s[c, r : r + step, :] * spec[:, lanes]).astype(BF16)
        filt = dot(scaled_s[...], qown[...]).astype(BF16).astype(F32)
        ids = tok if s == 0 else 3.0 - tok
        resid = jnp.broadcast_to(emb[:, 3:4], (dim, span))
        for t in range(3):
            resid = jnp.where(ids == float(t), emb[:, t : t + 1], resid)
        level = resid + filt
        level_s[:, here] = level
        scale = lax.rsqrt(jnp.sum(level * level, axis=0, keepdims=True) * (1.0 / dim) + 1e-06)
        m_s[:, here] = (level * scale * gmid).astype(BF16)
        normed = m_s[:, here]
        part = 256
        for h in range(0, hidden, part):
            gate = dot(w[h : h + part, :], normed).astype(BF16).astype(F32)
            up = dot(w[hidden + h : hidden + h + part, :], normed).astype(BF16).astype(F32)
            b = ba[h : h + part, here].astype(F32)
            sig = jax.nn.sigmoid(gate)
            swish = gate * sig
            act_s[h : h + part, here] = (swish * up).astype(BF16)
            bproj_s[h : h + part, here] = (b * up * sig * (1.0 + gate * (1.0 - sig))).astype(BF16)
            bproj_s[hidden + h : hidden + h + part, here] = (b * swish).astype(BF16)
        bmid = dot(wt[:, 0 : 2 * hidden], bproj_s[:, here]).astype(BF16).astype(F32)
        level = level_s[:, here]
        gmid_part += jnp.sum(bmid * level * scale, axis=1, keepdims=True)
        weighed = bmid * gmid
        pull = jnp.sum(weighed * level, axis=0, keepdims=True)
        dlevel = (
            bo[:, here].astype(F32)
            + scale * weighed
            - level * (scale * scale * scale * pull * (1.0 / dim))
        )
        df_s[:, here] = dlevel
        base = lax.broadcasted_iota(jnp.int32, (16, span), 0).astype(F32)
        mine = jnp.where(ids == base, 1.0, 0.0).astype(BF16)
        direct += dot_nt(dlevel.astype(BF16), mine)
    lane = lax.broadcasted_iota(jnp.int32, (dim, LANES), 1)
    small = jnp.where(lane == 4, gmid_part, 0.0)
    for t in range(4):
        small = jnp.where(lane == t, direct[:, t : t + 1], small)
    lanes = 2 * span // LANES
    fill = jnp.zeros((msg.shape[1] - (lanes + 1) * own_ch, LANES), F32)
    for sh in range(shards):
        rows = slice(sh * own_ch, (sh + 1) * own_ch)
        tiles = [df_s[rows, c * LANES : (c + 1) * LANES] for c in range(lanes)]
        msg[sh] = jnp.concatenate(tiles + [small[rows, :], fill], axis=0).astype(BF16)


def out_kernel(where_ref, level, act, bproj, m, bo, wt, out, keep, send, acc_s):
    dim, span = level.shape[0], level.shape[1] // 2
    hidden = act.shape[0]
    core = where_ref[1]
    for r in range(0, 2 * hidden, 256):
        acc_s[r : r + 256, :] = dot_nt(bproj[r : r + 256, :], m[...])
    for r in range(0, hidden, 256):
        acc_s[2 * hidden + r : 2 * hidden + r + 256, :] = dot_nt(act[r : r + 256, :], bo[...])
    chips, rows, _ = keep.shape
    pair = acc_s.shape[0] // chips
    for i in range(chips):
        keep[i] = acc_s[pl.ds(pl.multiple_of(i * pair + core * rows, 8), rows), :].astype(BF16)
        other = i * pair + (1 - core) * rows
        send[i] = acc_s[pl.ds(pl.multiple_of(other, 8), rows), :].astype(BF16)
    ri = lax.broadcasted_iota(jnp.int32, (dim, dim), 0)
    ci = lax.broadcasted_iota(jnp.int32, (dim, dim), 1)
    turn = jnp.where(ri + ci == dim - 1, 1.0, 0.0).astype(BF16)
    z = level[...] + dot(wt[:, 2 * hidden : 3 * hidden], act[...])
    z = z.astype(BF16)
    out[0:dim, :] = z[:, 0:span]
    out[dim : 2 * dim, :] = dot(turn, z[:, span : 2 * span]).astype(BF16)


def filter_kernel(msg, ohq, spec, lf, cols, escale_ref, qt, gf, small, *, span):
    shards = msg.shape[0]
    _, groups, _, group = ohq.shape
    own_ch = lf.shape[0]
    per_block = shards // groups
    lanes = span // LANES
    parts = [msg[sh].astype(F32) for sh in range(shards)]
    rows = []
    for s in range(2):
        for b in range(groups):
            tiles = []
            for q in range(per_block):
                x = parts[b * per_block + q]
                for h in range(lanes):
                    at = (s * lanes + h) * own_ch
                    tiles.append(x[at : at + own_ch, :])
            rows.append(jnp.concatenate(tiles, axis=1))
    df = jnp.concatenate(rows, axis=0).astype(BF16)
    ds = dot(df, qt[...]).astype(BF16).astype(F32)
    total = jnp.zeros((own_ch, group), F32)
    g = jnp.zeros((own_ch, 16), F32)
    for s in range(2):
        for b in range(groups):
            at = (s * groups + b) * own_ch
            d = ds[at : at + own_ch, :]
            total += d * spec[at : at + own_ch, :].astype(BF16).astype(F32)
            both = dot_nt((lf[...] * d).astype(BF16), ohq[s, b, 16:48, :])
            g += both[:, 0:16] + both[:, 16:32]
    for c in range(group // LANES):
        gf[c * own_ch : (c + 1) * own_ch, :] = total[:, c * LANES : (c + 1) * LANES]
    emb = cols[:, 0:4]
    taps = cols[:, 4:8]
    ntab = cols[:, 8:12]
    gin = cols[:, 12:13]
    escale = escale_ref[...]
    dn = jnp.zeros((own_ch, 4), F32)
    conv = []
    for k in range(4):
        gk = g[:, 4 * k : 4 * k + 4]
        dn += taps[:, k : k + 1] * gk
        conv.append(jnp.sum(ntab * gk, axis=1, keepdims=True))
    at = 2 * lanes * own_ch
    direct = parts[0][at : at + own_ch, :]
    for sh in range(1, shards):
        direct += parts[sh][at : at + own_ch, :]
    demb = escale * gin * dn + direct[:, 0:4]
    dgin = jnp.sum(dn * emb * escale, axis=1, keepdims=True)
    pull = jnp.sum(gin * dn * emb, axis=0, keepdims=True)
    lane = lax.broadcasted_iota(jnp.int32, (own_ch, LANES), 1)
    values = [demb[:, t : t + 1] for t in range(4)] + [dgin] + conv + [direct[:, 4:5]]
    table = jnp.zeros((own_ch, LANES), F32)
    for i, val in enumerate(values):
        table = jnp.where(lane == i, val, table)
    lane1 = lax.broadcasted_iota(jnp.int32, (8, LANES), 1)
    last = jnp.zeros((8, LANES), F32)
    for t in range(4):
        last = jnp.where(lane1 == t, pull[:, t : t + 1], last)
    small[0:own_ch, :] = table
    small[own_ch : own_ch + 8, :] = last


def to_all(x, axis):
    size = lax.axis_size(axis)
    return lax.all_to_all(jnp.broadcast_to(x[None], (size, *x.shape)), axis, 0, 0, tiled=True)


def split_to(x, axis):
    return lax.all_to_all(x, axis, 0, 0, tiled=True)


def swapped(x, axis, distance):
    return lax.ppermute(x, axis, [(i, i ^ distance) for i in range(lax.axis_size(axis))])


def added(a, b):
    return (a.astype(F32) + b.astype(F32)).astype(BF16)


def halved(parts, axis, distance, dim):
    bit = (lax.axis_index(axis) // distance) % 2
    sent = lax.dynamic_index_in_dim(parts, 1 - bit, dim, keepdims=False)
    kept = lax.dynamic_index_in_dim(parts, bit, dim, keepdims=False)
    return added(kept, swapped(sent, axis, distance))


def kernel_call(body, outs, ins, scratch=(), smem=0, flops=0, name=None):
    vmem = pl.BlockSpec(memory_space=pltpu.VMEM)
    moved = sum(x.size * x.dtype.itemsize for x in ins)
    moved += sum(int(np.prod(o.shape)) * o.dtype.itemsize for o in outs)
    return pl.pallas_call(
        body,
        out_shape=tuple(outs),
        in_specs=[pl.BlockSpec(memory_space=pltpu.SMEM)] * smem + [vmem] * (len(ins) - smem),
        out_specs=tuple([vmem] * len(outs)),
        scratch_shapes=list(scratch),
        compiler_params=pltpu.CompilerParams(vmem_limit_bytes=48 * 1024 * 1024),
        cost_estimate=pl.CostEstimate(flops=flops, bytes_accessed=moved, transcendentals=0),
        name=name,
    )(*ins)


def on_device(tokens, embedding, gain_in, conv_taps, long_filter, gain_mid, mlp_weights, cotangent):
    span = tokens.shape[1]
    dim = embedding.shape[1]
    hidden = mlp_weights.shape[0] // 3
    own_ch, group = long_filter.shape
    shards = lax.axis_size(SEQ)
    dps = lax.axis_size(DP)
    ys, xs = lax.axis_size("dp_y"), lax.axis_size("dp_x")
    chips = ys * xs
    per_block = group // span
    groups = shards // per_block
    chunks = group // LANES
    half = chunks // 2
    place = lax.axis_index(SEQ)
    core = lax.axis_index("dp_c")
    shape = jax.ShapeDtypeStruct

    mine = lax.dynamic_slice_in_dim(long_filter, core * half * LANES, half * LANES, 1)
    body = jnp.swapaxes(mine.astype(BF16).reshape(own_ch, half, LANES), 0, 1)
    ids = tokens.astype(BF16).reshape(span // LANES, LANES)
    msg = jnp.concatenate(
        [body.reshape(half * own_ch, LANES), jnp.pad(ids, ((0, 16 - span // LANES), (0, 0)))]
    )
    gath = to_all(msg, SEQ)
    gath_other = swapped(gath, "dp_c", 1)

    table = dct_table(group)
    qt = jnp.asarray(np.ascontiguousarray(table.T))
    qown = lax.dynamic_slice_in_dim(jnp.asarray(table), (place % per_block) * span, span, 1)
    emb_t = embedding.T
    escale = lax.rsqrt(jnp.mean(emb_t * emb_t, axis=0, keepdims=True) + 1e-06)
    ntab = (emb_t * escale * gain_in[:, None]).astype(BF16).astype(F32)
    coef = (conv_taps[:, :, None] * ntab[:, None, :]).reshape(dim, 16)
    chigh = coef.astype(BF16)
    clow = (coef - chigh.astype(F32)).astype(BF16)
    acat = jnp.concatenate([chigh, clow, chigh], axis=1)
    cols = jnp.concatenate(
        [emb_t, conv_taps, ntab, gain_in[:, None], gain_mid[:, None], jnp.zeros((dim, 2), F32)], axis=1
    )
    where = jnp.stack([place, core, place // per_block]).astype(jnp.int32)
    wt = mlp_weights.T
    acat_own = lax.dynamic_slice_in_dim(acat, place * own_ch, own_ch, 0)
    cols_own = lax.dynamic_slice_in_dim(cols, place * own_ch, own_ch, 0)

    bo, ba = kernel_call(
        back_kernel,
        [shape((dim, 2 * span), BF16), shape((hidden, 2 * span), BF16)],
        [cotangent[0], mlp_weights[2 * hidden :]],
        flops=4 * hidden * dim * span,
        name="back",
    )
    ohq, spec_own = kernel_call(
        partial(dct_kernel, half_rows=half * own_ch, per_block=per_block),
        [shape((2, groups, 48, group), BF16), shape((2 * groups * own_ch, group), F32)],
        [gath, acat_own, qt],
        flops=2 * 128 * group * group,
        name="bases",
    )
    lanes = 2 * span // LANES
    msg_rows = (lanes + 1) * own_ch
    msg_rows += -msg_rows % 16
    df_msg, m, act, bproj, level = kernel_call(
        mid_kernel,
        [
            shape((shards, msg_rows, LANES), BF16),
            shape((dim, 2 * span), BF16),
            shape((hidden, 2 * span), BF16),
            shape((2 * hidden, 2 * span), BF16),
            shape((dim, 2 * span), F32),
        ],
        [where, gath, gath_other, tokens, cols, acat, mlp_weights, wt, qown, ohq, bo, ba],
        scratch=[
            pltpu.VMEM((chunks, dim, LANES), F32),
            pltpu.VMEM((dim, group), BF16),
            pltpu.VMEM((dim, 2 * span), F32),
        ],
        smem=1,
        flops=12 * hidden * dim * span,
        name="mid",
    )
    df_parts = split_to(df_msg, SEQ)
    own_rows = 3 * hidden // dps
    layer, keep, send = kernel_call(
        out_kernel,
        [
            shape((2 * dim, span), BF16),
            shape((chips, own_rows, dim), BF16),
            shape((chips, own_rows, dim), BF16),
        ],
        [where, level, act, bproj, m, bo, wt],
        scratch=[pltpu.VMEM((3 * hidden, dim), F32)],
        smem=1,
        flops=16 * hidden * dim * span,
        name="out",
    )
    block = added(keep, swapped(send, "dp_c", 1))
    distance = 1
    block = block.reshape(ys, xs, own_rows, dim)
    while distance < ys:
        block = block.reshape(ys // (2 * distance), 2, *block.shape[1:])
        block = halved(block, "dp_y", distance, 1)
        if distance == 1 and xs == 2:
            block = halved(block, "dp_x", 1, 1)
        distance *= 2
    block = block.reshape(own_rows, dim)

    gf, small = kernel_call(
        partial(filter_kernel, span=span),
        [shape((chunks * own_ch, LANES), F32), shape((own_ch + 8, LANES), F32)],
        [df_parts, ohq, spec_own, long_filter, cols_own, escale, qt],
        flops=4 * groups * own_ch * group * group,
        name="filter",
    )
    small_n = 10
    flat = jnp.concatenate([small[:own_ch, :small_n].T.reshape(-1), small[own_ch, :4]])
    small_len = 256
    flat = jnp.pad(flat, (0, small_len - flat.shape[0]))
    piece = chunks * own_ch * LANES // dps
    packed = jnp.concatenate(
        [gf.reshape(dps, piece), jnp.broadcast_to(flat[None], (dps, small_len))], axis=1
    ).astype(BF16)
    packed = packed.reshape(dps, (piece + small_len) // LANES, LANES)
    summed = split_to(packed, DP).astype(F32).sum(0).reshape(-1)
    whole = to_all(summed[:piece].astype(BF16).reshape(piece // LANES, LANES), DP)
    grad_filter = (
        jnp.swapaxes(whole.astype(F32).reshape(chunks, own_ch, LANES), 0, 1).reshape(own_ch, group)
    )
    cols_each = dim // shards
    blocks = jnp.swapaxes(block.reshape(own_rows, shards, cols_each), 0, 1).reshape(shards, -1)
    smalls = jnp.broadcast_to(summed[piece:].astype(BF16)[None], (shards, small_len))
    final = jnp.concatenate([blocks, smalls], axis=1)
    final = jnp.pad(final, ((0, 0), (0, -final.shape[1] % 1024)))
    final = split_to(final.reshape(shards, -1, LANES), SEQ).astype(F32).reshape(shards, -1)
    grad_mlp = final[:, : own_rows * cols_each].sum(0).reshape(own_rows, cols_each)
    at = own_rows * cols_each
    everyone = final[:, at : at + small_n * own_ch].reshape(shards, small_n, own_ch)
    everyone = jnp.swapaxes(everyone, 0, 1).reshape(small_n, dim)
    pull = final[:, at + small_n * own_ch : at + small_n * own_ch + 4].sum(0)
    factor = escale[0] * escale[0] * escale[0] * pull * (1.0 / dim)
    grad_embedding = everyone[0:4] - embedding * factor[:, None]
    grad_gain_in = everyone[4]
    grad_conv = everyone[5:9].T
    grad_gain_mid = everyone[9]
    return layer[None], grad_embedding, grad_gain_in, grad_conv, grad_filter, grad_gain_mid, grad_mlp


def solution(mesh):
    dps, seqs = mesh.devices.shape
    cores = 2
    across = 2 if dps > 2 else 1
    torus = Mesh(
        mesh.devices.reshape(dps // (across * cores), across, cores, seqs // 2, 2), DP + SEQ
    )
    return jax.shard_map(
        on_device,
        mesh=torus,
        in_specs=(P(DP, SEQ), P(), P(), P(), P(SEQ, None), P(), P(), P(DP, None, SEQ)),
        out_specs=(P(DP, None, SEQ), P(), P(), P(), P(SEQ, None), P(), P(DP, SEQ)),
        check_vma=False,
    )
```

```python
from functools import partial

import jax
import jax.numpy as jnp
import numpy as np
from jax import lax
from jax.experimental import pallas as pl
from jax.experimental.pallas import tpu as pltpu
from jax.sharding import Mesh
from jax.sharding import PartitionSpec as P

DP = ("dp_y", "dp_x", "dp_c")
SEQ = ("seq_z", "seq_x")
F32, BF16 = jnp.float32, jnp.bfloat16
LANES = 128


def dct_table(length):
    freq = np.arange(length, dtype=np.int64)[:, None]
    place = np.arange(length, dtype=np.int64)[None, :]
    phase = (2 * place + 1) * freq % (4 * length)
    weight = np.where(freq == 0, np.sqrt(1.0 / length), np.sqrt(2.0 / length))
    return (weight * np.cos(np.pi * phase / (2 * length))).astype(np.float32).astype(jnp.bfloat16)


def dot(a, b):
    return jnp.dot(a, b, preferred_element_type=F32)


def dot_nt(a, b):
    return lax.dot_general(a, b, (((1,), (1,)), ((), ())), preferred_element_type=F32)


def onehot_rows(gath, groups, group, half_rows, per_block):
    shards = gath.shape[0]
    rows_of = 2
    ids = [gath[sh, half_rows : half_rows + 16, :].astype(F32) for sh in range(shards)]
    rows = [ids[sh][j : j + 1, :] for sh in range(shards) for j in range(rows_of)]
    outside = jnp.full((1, LANES), -1.0, F32)
    rows = [outside] + rows + [outside]
    per = per_block * rows_of
    width = group + 2 * LANES
    row = lax.broadcasted_iota(jnp.int32, (32, group), 0)
    want = jnp.where(row < 16, row % 4, 3 - row % 4).astype(F32)
    onehots = []
    for b in range(groups):
        pieces = rows[b * per : b * per + per + 2]
        ext = jnp.concatenate([jnp.broadcast_to(p, (8, LANES)) for p in pieces], axis=1)
        picked = jnp.zeros((32, group), F32)
        for j in range(8):
            shift = j if j < 4 else (width - (j - 4)) % width
            moved = ext if shift == 0 else pltpu.roll(ext, shift, 1)
            moved = jnp.broadcast_to(moved[0:1, LANES : LANES + group], (32, group))
            picked = jnp.where(row // 4 == j, moved, picked)
        onehots.append(jnp.where(picked == want, 1.0, 0.0).astype(BF16))
    return onehots


def dct_kernel(gath, acat, qt, ohq, spec, *, half_rows, per_block):
    own_ch = acat.shape[0]
    _, groups, _, group = ohq.shape
    onehots = onehot_rows(gath, groups, group, half_rows, per_block)
    both = dot(jnp.concatenate(onehots, axis=0), qt[...])
    for b in range(groups):
        x = both[32 * b : 32 * b + 32, :]
        high = x.astype(BF16)
        low = (x - high.astype(F32)).astype(BF16)
        for s in range(2):
            o_high = high[16 * s : 16 * s + 16]
            o_low = low[16 * s : 16 * s + 16]
            ocat = jnp.concatenate([o_high, o_high, o_low], axis=0)
            ohq[s, b] = ocat
            at = (s * groups + b) * own_ch
            spec[at : at + own_ch, :] = dot(acat[...], ocat)


def back_kernel(cot, w_down, bo, ba):
    dim, span = cot.shape[0] // 2, cot.shape[1]
    ri = lax.broadcasted_iota(jnp.int32, (dim, dim), 0)
    ci = lax.broadcasted_iota(jnp.int32, (dim, dim), 1)
    turn = jnp.where(ri + ci == dim - 1, 1.0, 0.0).astype(BF16)
    bo[:, 0:span] = cot[0:dim, :]
    bo[:, span : 2 * span] = dot(turn, cot[dim : 2 * dim, :]).astype(BF16)
    for r in range(0, w_down.shape[0], 256):
        ba[r : r + 256, :] = dot(w_down[r : r + 256, :], bo[...]).astype(BF16)


def mid_kernel(
    where_ref, ga, gb, tok_ref, cols, acat, w, wt, qown, ohq, bo, ba,
    msg, act_s, level_s, keep, send,
    lf_s, scaled_s, df_s, m_s, bproj_s, acc_s,
):
    shards = ga.shape[0]
    chunks, dim, _ = lf_s.shape
    own_ch = dim // shards
    hidden = act_s.shape[0]
    span = tok_ref.shape[1]
    half = chunks // 2
    body_rows = half * own_ch
    core = where_ref[1]
    block = where_ref[2]
    for sh in range(shards):
        for c in range(half):
            rows = slice(c * own_ch, (c + 1) * own_ch)
            dst = slice(sh * own_ch, (sh + 1) * own_ch)
            lf_s[core * half + c, dst, :] = ga[sh, 0:body_rows, :].astype(F32)[rows, :]
            lf_s[(1 - core) * half + c, dst, :] = gb[sh, 0:body_rows, :].astype(F32)[rows, :]
    emb = cols[:, 0:4]
    gmid = cols[:, 13:14]
    tok = tok_ref[...].astype(F32)
    step = 128
    gmid_part = jnp.zeros((dim, 1), F32)
    direct = jnp.zeros((dim, 16), F32)
    for s in range(2):
        here = slice(s * span, (s + 1) * span)
        ocat = ohq[s, block]
        for r in range(0, dim, step):
            spec = dot(acat[r : r + step, :], ocat).astype(BF16).astype(F32)
            for c in range(chunks):
                lanes = slice(c * LANES, (c + 1) * LANES)
                scaled_s[r : r + step, lanes] = (lf_s[c, r : r + step, :] * spec[:, lanes]).astype(BF16)
        filt = dot(scaled_s[...], qown[...]).astype(BF16).astype(F32)
        ids = tok if s == 0 else 3.0 - tok
        resid = jnp.broadcast_to(emb[:, 3:4], (dim, span))
        for t in range(3):
            resid = jnp.where(ids == float(t), emb[:, t : t + 1], resid)
        level = resid + filt
        level_s[:, here] = level
        scale = lax.rsqrt(jnp.sum(level * level, axis=0, keepdims=True) * (1.0 / dim) + 1e-06)
        m_s[:, here] = (level * scale * gmid).astype(BF16)
        normed = m_s[:, here]
        part = 256
        for h in range(0, hidden, part):
            gate = dot(w[h : h + part, :], normed).astype(BF16).astype(F32)
            up = dot(w[hidden + h : hidden + h + part, :], normed).astype(BF16).astype(F32)
            b = ba[h : h + part, here].astype(F32)
            sig = jax.nn.sigmoid(gate)
            swish = gate * sig
            act_s[h : h + part, here] = (swish * up).astype(BF16)
            bproj_s[h : h + part, here] = (b * up * sig * (1.0 + gate * (1.0 - sig))).astype(BF16)
            bproj_s[hidden + h : hidden + h + part, here] = (b * swish).astype(BF16)
        bmid = dot(wt[:, 0 : 2 * hidden], bproj_s[:, here]).astype(BF16).astype(F32)
        level = level_s[:, here]
        gmid_part += jnp.sum(bmid * level * scale, axis=1, keepdims=True)
        weighed = bmid * gmid
        pull = jnp.sum(weighed * level, axis=0, keepdims=True)
        dlevel = (
            bo[:, here].astype(F32)
            + scale * weighed
            - level * (scale * scale * scale * pull * (1.0 / dim))
        )
        df_s[:, here] = dlevel
        base = lax.broadcasted_iota(jnp.int32, (16, span), 0).astype(F32)
        mine = jnp.where(ids == base, 1.0, 0.0).astype(BF16)
        direct += dot_nt(dlevel.astype(BF16), mine)
    lane = lax.broadcasted_iota(jnp.int32, (dim, LANES), 1)
    small = jnp.where(lane == 4, gmid_part, 0.0)
    for t in range(4):
        small = jnp.where(lane == t, direct[:, t : t + 1], small)
    lanes = 2 * span // LANES
    fill = jnp.zeros((msg.shape[1] - (lanes + 1) * own_ch, LANES), F32)
    for sh in range(shards):
        rows = slice(sh * own_ch, (sh + 1) * own_ch)
        tiles = [df_s[rows, c * LANES : (c + 1) * LANES] for c in range(lanes)]
        msg[sh] = jnp.concatenate(tiles + [small[rows, :], fill], axis=0).astype(BF16)
    for r in range(0, 2 * hidden, 256):
        acc_s[r : r + 256, :] = dot_nt(bproj_s[r : r + 256, :], m_s[...])
    for r in range(0, hidden, 256):
        acc_s[2 * hidden + r : 2 * hidden + r + 256, :] = dot_nt(act_s[r : r + 256, :], bo[...])
    chips, rows, _ = keep.shape
    pair = acc_s.shape[0] // chips
    for i in range(chips):
        keep[i] = acc_s[pl.ds(pl.multiple_of(i * pair + core * rows, 8), rows), :].astype(BF16)
        other = i * pair + (1 - core) * rows
        send[i] = acc_s[pl.ds(pl.multiple_of(other, 8), rows), :].astype(BF16)


def out_kernel(level, act, wt, out):
    dim, span = level.shape[0], level.shape[1] // 2
    hidden = act.shape[0]
    ri = lax.broadcasted_iota(jnp.int32, (dim, dim), 0)
    ci = lax.broadcasted_iota(jnp.int32, (dim, dim), 1)
    turn = jnp.where(ri + ci == dim - 1, 1.0, 0.0).astype(BF16)
    z = level[...] + dot(wt[:, 2 * hidden : 3 * hidden], act[...])
    z = z.astype(BF16)
    out[0:dim, :] = z[:, 0:span]
    out[dim : 2 * dim, :] = dot(turn, z[:, span : 2 * span]).astype(BF16)


def gather_kernel(where_ref, lf, tok, msg):
    own_ch, group = lf.shape
    half = group // LANES // 2
    core = where_ref[1]
    tiles = []
    for c in range(half):
        at = pl.multiple_of((core * half + c) * LANES, LANES)
        tiles.append(lf[:, pl.ds(at, LANES)])
    ids = jnp.broadcast_to(tok[...].astype(F32), (8, tok.shape[1]))
    row = lax.broadcasted_iota(jnp.int32, (16, LANES), 0)
    last = jnp.zeros((16, LANES), F32)
    for j in range(tok.shape[1] // LANES):
        part = jnp.broadcast_to(ids[0:1, j * LANES : (j + 1) * LANES], (16, LANES))
        last = jnp.where(row == j, part, last)
    whole = jnp.concatenate(tiles + [last], axis=0).astype(BF16)
    for sh in range(msg.shape[0]):
        msg[sh] = whole


def split_kernel(where_ref, keep, came, kept, sent, *, xs):
    bit = where_ref[3]
    for i in range(kept.shape[0]):
        high, low = i // xs, i % xs
        one = (high * 2 + bit) * xs + low
        two = (high * 2 + 1 - bit) * xs + low
        kept[i] = (keep[one].astype(F32) + came[one].astype(F32)).astype(BF16)
        sent[i] = (keep[two].astype(F32) + came[two].astype(F32)).astype(BF16)


def pack_kernel(kept, came, sums, msg):
    rows, dim = kept.shape
    shards = msg.shape[0]
    own = dim // shards
    block = kept[...].astype(F32) + came[...].astype(F32)
    block = jnp.concatenate([block, jnp.zeros((LANES - rows, dim), F32)], axis=0).T
    lane = lax.broadcasted_iota(jnp.int32, (16, LANES), 1)
    row = lax.broadcasted_iota(jnp.int32, (16, LANES), 0)
    small = jnp.where(lane < own + 4, pltpu.roll(sums[...], 10, 0), 0.0)
    small = jnp.where(row < 10, pltpu.roll(small, 96, 1), 0.0)
    small = jnp.concatenate([small, jnp.zeros((own - 16, LANES), F32)], axis=0)
    fill = jnp.zeros((msg.shape[1] - own, LANES), F32)
    for sh in range(shards):
        part = block[sh * own : (sh + 1) * own, :] + small
        msg[sh] = jnp.concatenate([part, fill], axis=0).astype(BF16)


def final_kernel(got, emb, escale, g_mlp, g_emb, g_gin, g_conv, g_mid):
    shards = got.shape[0]
    rows, own = g_mlp.shape
    dim = emb.shape[1]
    lane = lax.broadcasted_iota(jnp.int32, (16, LANES), 1)
    total = jnp.zeros(got.shape[1:], F32)
    acc = jnp.zeros((16, dim), F32)
    for sh in range(shards):
        x = got[sh].astype(F32)
        total += x
        y = jnp.where((lane >= 96) & (lane < 96 + own), x[0:16, :], 0.0)
        wide = jnp.concatenate([y, jnp.zeros((16, dim - LANES), F32)], axis=1)
        shift = (sh * own - 96) % dim
        acc += wide if shift == 0 else pltpu.roll(wide, shift, 1)
    turned = jnp.concatenate([total, jnp.zeros((LANES - got.shape[1], LANES), F32)], axis=0).T
    g_mlp[...] = turned[0:rows, 0:own]
    at = 96 + own
    pull = turned[at : at + 4, 0:1]
    e = escale[...]
    g_emb[...] = acc[0:4, :] - emb[...] * (e * e * e * pull * (1.0 / dim))
    g_gin[...] = acc[4:5, :]
    g_mid[...] = acc[9:10, :]
    flipped = jnp.concatenate([acc, jnp.zeros((LANES - 16, dim), F32)], axis=0).T
    g_conv[...] = flipped[:, 5:9]


def filter_kernel(msg, ohq, spec, lf, cols, escale_ref, qt, packed, gf, *, span):
    shards = msg.shape[0]
    _, groups, _, group = ohq.shape
    own_ch = lf.shape[0]
    per_block = shards // groups
    lanes = span // LANES
    parts = [msg[sh].astype(F32) for sh in range(shards)]
    rows = []
    for s in range(2):
        for b in range(groups):
            tiles = []
            for q in range(per_block):
                x = parts[b * per_block + q]
                for h in range(lanes):
                    at = (s * lanes + h) * own_ch
                    tiles.append(x[at : at + own_ch, :])
            rows.append(jnp.concatenate(tiles, axis=1))
    df = jnp.concatenate(rows, axis=0).astype(BF16)
    ds = dot(df, qt[...]).astype(BF16).astype(F32)
    total = jnp.zeros((own_ch, group), F32)
    g = jnp.zeros((own_ch, 16), F32)
    for s in range(2):
        for b in range(groups):
            at = (s * groups + b) * own_ch
            d = ds[at : at + own_ch, :]
            total += d * spec[at : at + own_ch, :].astype(BF16).astype(F32)
            both = dot_nt((lf[...] * d).astype(BF16), ohq[s, b, 16:48, :])
            g += both[:, 0:16] + both[:, 16:32]
    for c in range(group // LANES):
        gf[c * own_ch : (c + 1) * own_ch, :] = total[:, c * LANES : (c + 1) * LANES]
    emb = cols[:, 0:4]
    taps = cols[:, 4:8]
    ntab = cols[:, 8:12]
    gin = cols[:, 12:13]
    escale = escale_ref[...]
    dn = jnp.zeros((own_ch, 4), F32)
    conv = []
    for k in range(4):
        gk = g[:, 4 * k : 4 * k + 4]
        dn += taps[:, k : k + 1] * gk
        conv.append(jnp.sum(ntab * gk, axis=1, keepdims=True))
    at = 2 * lanes * own_ch
    direct = parts[0][at : at + own_ch, :]
    for sh in range(1, shards):
        direct += parts[sh][at : at + own_ch, :]
    demb = escale * gin * dn + direct[:, 0:4]
    dgin = jnp.sum(dn * emb * escale, axis=1, keepdims=True)
    pull = jnp.sum(gin * dn * emb, axis=0, keepdims=True)
    lane = lax.broadcasted_iota(jnp.int32, (own_ch, LANES), 1)
    values = [demb[:, t : t + 1] for t in range(4)] + [dgin] + conv + [direct[:, 4:5]]
    table = jnp.zeros((own_ch, LANES), F32)
    for i, val in enumerate(values):
        table = jnp.where(lane == i, val, table)
    square = jnp.concatenate([table, jnp.zeros((LANES - own_ch, LANES), F32)], axis=0).T
    small = square[0:16, :]
    lane = lax.broadcasted_iota(jnp.int32, (16, LANES), 1)
    row = lax.broadcasted_iota(jnp.int32, (16, LANES), 0)
    for t in range(4):
        value = jnp.broadcast_to(pull[:, t : t + 1], (16, LANES))
        small = jnp.where((row == 0) & (lane == own_ch + t), value, small)
    small = pltpu.roll(small, 6, 0)
    peers = packed.shape[0]
    piece = group // LANES * own_ch // peers
    for i in range(peers):
        at = min(i * piece // 8 * 8, group // LANES * own_ch - 16)
        block = gf[at : at + 16, :]
        off = i * piece - at
        if off:
            block = pltpu.roll(block, 16 - off, 0)
        packed[i] = jnp.where(row < piece, block, small).astype(BF16)


def to_all(x, axis):
    size = lax.axis_size(axis)
    return lax.all_to_all(jnp.broadcast_to(x[None], (size, *x.shape)), axis, 0, 0, tiled=True)


def split_to(x, axis):
    return lax.all_to_all(x, axis, 0, 0, tiled=True)


def swapped(x, axis, distance):
    return lax.ppermute(x, axis, [(i, i ^ distance) for i in range(lax.axis_size(axis))])


def added(a, b):
    return (a.astype(F32) + b.astype(F32)).astype(BF16)


def halved(parts, axis, distance, dim):
    bit = (lax.axis_index(axis) // distance) % 2
    sent = lax.dynamic_index_in_dim(parts, 1 - bit, dim, keepdims=False)
    kept = lax.dynamic_index_in_dim(parts, bit, dim, keepdims=False)
    return kept, swapped(sent, axis, distance)


def kernel_call(body, outs, ins, scratch=(), smem=0, flops=0, name=None):
    vmem = pl.BlockSpec(memory_space=pltpu.VMEM)
    moved = sum(x.size * x.dtype.itemsize for x in ins)
    moved += sum(int(np.prod(o.shape)) * o.dtype.itemsize for o in outs)
    return pl.pallas_call(
        body,
        out_shape=tuple(outs),
        in_specs=[pl.BlockSpec(memory_space=pltpu.SMEM)] * smem + [vmem] * (len(ins) - smem),
        out_specs=tuple([vmem] * len(outs)),
        scratch_shapes=list(scratch),
        compiler_params=pltpu.CompilerParams(vmem_limit_bytes=48 * 1024 * 1024),
        cost_estimate=pl.CostEstimate(flops=flops, bytes_accessed=moved, transcendentals=0),
        name=name,
    )(*ins)


def on_device(tokens, embedding, gain_in, conv_taps, long_filter, gain_mid, mlp_weights, cotangent):
    span = tokens.shape[1]
    dim = embedding.shape[1]
    hidden = mlp_weights.shape[0] // 3
    own_ch, group = long_filter.shape
    shards = lax.axis_size(SEQ)
    dps = lax.axis_size(DP)
    ys, xs = lax.axis_size("dp_y"), lax.axis_size("dp_x")
    chips = ys * xs
    per_block = group // span
    groups = shards // per_block
    chunks = group // LANES
    half = chunks // 2
    place = lax.axis_index(SEQ)
    core = lax.axis_index("dp_c")
    shape = jax.ShapeDtypeStruct

    vec = jnp.stack([place, core, place // per_block, lax.axis_index("dp_y") % 2])
    where = vec.astype(jnp.int32)
    (msg,) = kernel_call(
        gather_kernel,
        [shape((shards, half * own_ch + 16, LANES), BF16)],
        [where, long_filter, tokens],
        smem=1,
        name="gather",
    )
    gath = split_to(msg, SEQ)

    table = dct_table(group)
    qt = jnp.asarray(np.ascontiguousarray(table.T))
    qown = lax.dynamic_slice_in_dim(jnp.asarray(table), (place % per_block) * span, span, 1)
    emb_t = embedding.T
    escale = lax.rsqrt(jnp.mean(emb_t * emb_t, axis=0, keepdims=True) + 1e-06)
    ntab = (emb_t * escale * gain_in[:, None]).astype(BF16).astype(F32)
    coef = (conv_taps[:, :, None] * ntab[:, None, :]).reshape(dim, 16)
    chigh = coef.astype(BF16)
    clow = (coef - chigh.astype(F32)).astype(BF16)
    acat = jnp.concatenate([chigh, clow, chigh], axis=1)
    cols = jnp.concatenate(
        [emb_t, conv_taps, ntab, gain_in[:, None], gain_mid[:, None], jnp.zeros((dim, 2), F32)], axis=1
    )
    wt = mlp_weights.T
    acat_own = lax.dynamic_slice_in_dim(acat, place * own_ch, own_ch, 0)
    cols_own = lax.dynamic_slice_in_dim(cols, place * own_ch, own_ch, 0)

    bo, ba = kernel_call(
        back_kernel,
        [shape((dim, 2 * span), BF16), shape((hidden, 2 * span), BF16)],
        [cotangent[0], mlp_weights[2 * hidden :]],
        flops=4 * hidden * dim * span,
        name="back",
    )
    gath, bo, ba, wt, qown, acat, cols, acat_own, cols_own = lax.optimization_barrier(
        (gath, bo, ba, wt, qown, acat, cols, acat_own, cols_own)
    )
    gath_other = swapped(gath, "dp_c", 1)
    ohq, spec_own = kernel_call(
        partial(dct_kernel, half_rows=half * own_ch, per_block=per_block),
        [shape((2, groups, 48, group), BF16), shape((2 * groups * own_ch, group), F32)],
        [gath, acat_own, qt],
        flops=2 * 128 * group * group,
        name="bases",
    )
    lanes = 2 * span // LANES
    msg_rows = (lanes + 1) * own_ch
    msg_rows += -msg_rows % 16
    own_rows = 3 * hidden // dps
    df_msg, act, level, keep, send = kernel_call(
        mid_kernel,
        [
            shape((shards, msg_rows, LANES), BF16),
            shape((hidden, 2 * span), BF16),
            shape((dim, 2 * span), F32),
            shape((chips, own_rows, dim), BF16),
            shape((chips, own_rows, dim), BF16),
        ],
        [where, gath, gath_other, tokens, cols, acat, mlp_weights, wt, qown, ohq, bo, ba],
        scratch=[
            pltpu.VMEM((chunks, dim, LANES), F32),
            pltpu.VMEM((dim, group), BF16),
            pltpu.VMEM((dim, 2 * span), F32),
            pltpu.VMEM((dim, 2 * span), BF16),
            pltpu.VMEM((2 * hidden, 2 * span), BF16),
            pltpu.VMEM((3 * hidden, dim), F32),
        ],
        smem=1,
        flops=12 * hidden * dim * span,
        name="mid",
    )
    df_parts = split_to(df_msg, SEQ)
    (layer,) = kernel_call(
        out_kernel, [shape((2 * dim, span), BF16)], [level, act, wt], flops=4 * hidden * dim * span, name="out"
    )
    kept, sent = kernel_call(
        partial(split_kernel, xs=xs),
        [shape((chips // 2, own_rows, dim), BF16)] * 2,
        [where, keep, swapped(send, "dp_c", 1)],
        smem=1,
        name="split",
    )
    block = added(kept, swapped(sent, "dp_y", 1)).reshape(ys // 2, xs, own_rows, dim)
    kept, came = halved(block, "dp_x", 1, 1)
    distance = 2
    while distance < ys:
        block = added(kept, came).reshape(ys // (2 * distance), 2, own_rows, dim)
        kept, came = halved(block, "dp_y", distance, 1)
        distance *= 2
    kept, came = kept.reshape(own_rows, dim), came.reshape(own_rows, dim)

    piece = chunks * own_ch // dps
    (packed,) = kernel_call(
        partial(filter_kernel, span=span),
        [shape((dps, 16, LANES), BF16)],
        [df_parts, ohq, spec_own, long_filter, cols_own, escale, qt],
        scratch=[pltpu.VMEM((chunks * own_ch, LANES), F32)],
        flops=4 * groups * own_ch * group * group,
        name="filter",
    )
    summed = split_to(packed, DP).astype(F32).sum(0)
    whole = to_all(summed[:piece].astype(BF16), DP)
    grad_filter = (
        jnp.swapaxes(whole.astype(F32).reshape(chunks, own_ch, LANES), 0, 1).reshape(own_ch, group)
    )
    cols_each = dim // shards
    (final,) = kernel_call(
        pack_kernel, [shape((shards, 32, LANES), BF16)], [kept, came, summed], name="pack"
    )
    final = split_to(final, SEQ)
    grad_mlp, grad_embedding, grad_gain_in, grad_conv, grad_gain_mid = kernel_call(
        final_kernel,
        [
            shape((own_rows, cols_each), F32),
            shape((4, dim), F32),
            shape((1, dim), F32),
            shape((dim, 4), F32),
            shape((1, dim), F32),
        ],
        [final, embedding, escale.reshape(4, 1)],
        name="final",
    )
    grad_gain_in, grad_gain_mid = grad_gain_in.reshape(dim), grad_gain_mid.reshape(dim)
    return layer[None], grad_embedding, grad_gain_in, grad_conv, grad_filter, grad_gain_mid, grad_mlp


def solution(mesh):
    dps, seqs = mesh.devices.shape
    cores = 2
    across = 2 if dps > 2 else 1
    torus = Mesh(
        mesh.devices.reshape(dps // (across * cores), across, cores, seqs // 2, 2), DP + SEQ
    )
    return jax.shard_map(
        on_device,
        mesh=torus,
        in_specs=(P(DP, SEQ), P(), P(), P(), P(SEQ, None), P(), P(), P(DP, None, SEQ)),
        out_specs=(P(DP, None, SEQ), P(), P(), P(), P(SEQ, None), P(), P(DP, SEQ)),
        check_vma=False,
    )
```

```python
from functools import partial

import jax
import jax.numpy as jnp
import numpy as np
from jax import lax
from jax.experimental import pallas as pl
from jax.experimental.pallas import tpu as pltpu
from jax.sharding import Mesh
from jax.sharding import PartitionSpec as P

DP = ("dp_y", "dp_n", "dp_x", "dp_c")
SEQ = ("seq_z", "seq_x")
LAST = ("dp_y",) + SEQ
F32, BF16 = jnp.float32, jnp.bfloat16
LANES = 128


def dct_table(length):
    freq = np.arange(length, dtype=np.int64)[:, None]
    place = np.arange(length, dtype=np.int64)[None, :]
    phase = (2 * place + 1) * freq % (4 * length)
    weight = np.where(freq == 0, np.sqrt(1.0 / length), np.sqrt(2.0 / length))
    return (weight * np.cos(np.pi * phase / (2 * length))).astype(np.float32).astype(jnp.bfloat16)


def dot(a, b):
    return jnp.dot(a, b, preferred_element_type=F32)


def dot_nt(a, b):
    return lax.dot_general(a, b, (((1,), (1,)), ((), ())), preferred_element_type=F32)


def onehot_rows(gath, groups, group, half_rows, per_block):
    shards = gath.shape[0]
    rows_of = 2
    ids = [gath[sh, half_rows : half_rows + 16, :].astype(F32) for sh in range(shards)]
    rows = [ids[sh][j : j + 1, :] for sh in range(shards) for j in range(rows_of)]
    outside = jnp.full((1, LANES), -1.0, F32)
    rows = [outside] + rows + [outside]
    per = per_block * rows_of
    width = group + 2 * LANES
    row = lax.broadcasted_iota(jnp.int32, (32, group), 0)
    want = jnp.where(row < 16, row % 4, 3 - row % 4).astype(F32)
    onehots = []
    for b in range(groups):
        pieces = rows[b * per : b * per + per + 2]
        ext = jnp.concatenate([jnp.broadcast_to(p, (8, LANES)) for p in pieces], axis=1)
        picked = jnp.zeros((32, group), F32)
        for j in range(8):
            shift = j if j < 4 else (width - (j - 4)) % width
            moved = ext if shift == 0 else pltpu.roll(ext, shift, 1)
            moved = jnp.broadcast_to(moved[0:1, LANES : LANES + group], (32, group))
            picked = jnp.where(row // 4 == j, moved, picked)
        onehots.append(jnp.where(picked == want, 1.0, 0.0).astype(BF16))
    return onehots


def dct_kernel(gath, acat, qt, ohq, spec, *, half_rows, per_block):
    own_ch = acat.shape[0]
    _, groups, _, group = ohq.shape
    onehots = onehot_rows(gath, groups, group, half_rows, per_block)
    both = dot(jnp.concatenate(onehots, axis=0), qt[...])
    for b in range(groups):
        x = both[32 * b : 32 * b + 32, :]
        high = x.astype(BF16)
        low = (x - high.astype(F32)).astype(BF16)
        for s in range(2):
            o_high = high[16 * s : 16 * s + 16]
            o_low = low[16 * s : 16 * s + 16]
            ocat = jnp.concatenate([o_high, o_high, o_low], axis=0)
            ohq[s, b] = ocat
            at = (s * groups + b) * own_ch
            spec[at : at + own_ch, :] = dot(acat[...], ocat)


def back_kernel(cot, w_down, bo, ba):
    dim, span = cot.shape[0] // 2, cot.shape[1]
    ri = lax.broadcasted_iota(jnp.int32, (dim, dim), 0)
    ci = lax.broadcasted_iota(jnp.int32, (dim, dim), 1)
    turn = jnp.where(ri + ci == dim - 1, 1.0, 0.0).astype(BF16)
    bo[:, 0:span] = cot[0:dim, :]
    bo[:, span : 2 * span] = dot(turn, cot[dim : 2 * dim, :]).astype(BF16)
    for r in range(0, w_down.shape[0], 256):
        ba[r : r + 256, :] = dot(w_down[r : r + 256, :], bo[...]).astype(BF16)


def mid_kernel(
    where_ref, ga, gb, tok_ref, cols, acat, w, wt, qown, ohq, bo, ba,
    msg, act_s, level_s, keep, send,
    lf_s, scaled_s, df_s, m_s, bproj_s, acc_s,
):
    shards = ga.shape[0]
    chunks, dim, _ = lf_s.shape
    own_ch = dim // shards
    hidden = act_s.shape[0]
    span = tok_ref.shape[1]
    half = chunks // 2
    body_rows = half * own_ch
    core = where_ref[1]
    block = where_ref[2]
    for sh in range(shards):
        for c in range(half):
            rows = slice(c * own_ch, (c + 1) * own_ch)
            dst = slice(sh * own_ch, (sh + 1) * own_ch)
            lf_s[core * half + c, dst, :] = ga[sh, 0:body_rows, :].astype(F32)[rows, :]
            lf_s[(1 - core) * half + c, dst, :] = gb[sh, 0:body_rows, :].astype(F32)[rows, :]
    emb = cols[:, 0:4]
    gmid = cols[:, 13:14]
    tok = tok_ref[...].astype(F32)
    step = 128
    gmid_part = jnp.zeros((dim, 1), F32)
    direct = jnp.zeros((dim, 16), F32)
    for s in range(2):
        here = slice(s * span, (s + 1) * span)
        ocat = ohq[s, block]
        for r in range(0, dim, step):
            spec = dot(acat[r : r + step, :], ocat).astype(BF16).astype(F32)
            for c in range(chunks):
                lanes = slice(c * LANES, (c + 1) * LANES)
                scaled_s[r : r + step, lanes] = (lf_s[c, r : r + step, :] * spec[:, lanes]).astype(BF16)
        filt = dot(scaled_s[...], qown[...]).astype(BF16).astype(F32)
        ids = tok if s == 0 else 3.0 - tok
        resid = jnp.broadcast_to(emb[:, 3:4], (dim, span))
        for t in range(3):
            resid = jnp.where(ids == float(t), emb[:, t : t + 1], resid)
        level = resid + filt
        level_s[:, here] = level
        scale = lax.rsqrt(jnp.sum(level * level, axis=0, keepdims=True) * (1.0 / dim) + 1e-06)
        m_s[:, here] = (level * scale * gmid).astype(BF16)
        normed = m_s[:, here]
        part = 256
        for h in range(0, hidden, part):
            gate = dot(w[h : h + part, :], normed).astype(BF16).astype(F32)
            up = dot(w[hidden + h : hidden + h + part, :], normed).astype(BF16).astype(F32)
            b = ba[h : h + part, here].astype(F32)
            sig = jax.nn.sigmoid(gate)
            swish = gate * sig
            act_s[h : h + part, here] = (swish * up).astype(BF16)
            bproj_s[h : h + part, here] = (b * up * sig * (1.0 + gate * (1.0 - sig))).astype(BF16)
            bproj_s[hidden + h : hidden + h + part, here] = (b * swish).astype(BF16)
        bmid = dot(wt[:, 0 : 2 * hidden], bproj_s[:, here]).astype(BF16).astype(F32)
        level = level_s[:, here]
        gmid_part += jnp.sum(bmid * level * scale, axis=1, keepdims=True)
        weighed = bmid * gmid
        pull = jnp.sum(weighed * level, axis=0, keepdims=True)
        dlevel = (
            bo[:, here].astype(F32)
            + scale * weighed
            - level * (scale * scale * scale * pull * (1.0 / dim))
        )
        df_s[:, here] = dlevel
        base = lax.broadcasted_iota(jnp.int32, (16, span), 0).astype(F32)
        mine = jnp.where(ids == base, 1.0, 0.0).astype(BF16)
        direct += dot_nt(dlevel.astype(BF16), mine)
    lane = lax.broadcasted_iota(jnp.int32, (dim, LANES), 1)
    small = jnp.where(lane == 4, gmid_part, 0.0)
    for t in range(4):
        small = jnp.where(lane == t, direct[:, t : t + 1], small)
    lanes = 2 * span // LANES
    fill = jnp.zeros((msg.shape[1] - (lanes + 1) * own_ch, LANES), F32)
    for sh in range(shards):
        rows = slice(sh * own_ch, (sh + 1) * own_ch)
        tiles = [df_s[rows, c * LANES : (c + 1) * LANES] for c in range(lanes)]
        msg[sh] = jnp.concatenate(tiles + [small[rows, :], fill], axis=0).astype(BF16)
    for r in range(0, 2 * hidden, 256):
        acc_s[r : r + 256, :] = dot_nt(bproj_s[r : r + 256, :], m_s[...])
    for r in range(0, hidden, 256):
        acc_s[2 * hidden + r : 2 * hidden + r + 256, :] = dot_nt(act_s[r : r + 256, :], bo[...])
    chips, rows, _ = keep.shape
    pair = acc_s.shape[0] // chips
    for i in range(chips):
        keep[i] = acc_s[pl.ds(pl.multiple_of(i * pair + core * rows, 8), rows), :].astype(BF16)
        other = i * pair + (1 - core) * rows
        send[i] = acc_s[pl.ds(pl.multiple_of(other, 8), rows), :].astype(BF16)


def out_kernel(level, act, wt, out):
    dim, span = level.shape[0], level.shape[1] // 2
    hidden = act.shape[0]
    ri = lax.broadcasted_iota(jnp.int32, (dim, dim), 0)
    ci = lax.broadcasted_iota(jnp.int32, (dim, dim), 1)
    turn = jnp.where(ri + ci == dim - 1, 1.0, 0.0).astype(BF16)
    z = level[...] + dot(wt[:, 2 * hidden : 3 * hidden], act[...])
    z = z.astype(BF16)
    out[0:dim, :] = z[:, 0:span]
    out[dim : 2 * dim, :] = dot(turn, z[:, span : 2 * span]).astype(BF16)


def gather_kernel(where_ref, lf, tok, msg):
    own_ch, group = lf.shape
    half = group // LANES // 2
    core = where_ref[1]
    tiles = []
    for c in range(half):
        at = pl.multiple_of((core * half + c) * LANES, LANES)
        tiles.append(lf[:, pl.ds(at, LANES)])
    ids = jnp.broadcast_to(tok[...].astype(F32), (8, tok.shape[1]))
    row = lax.broadcasted_iota(jnp.int32, (16, LANES), 0)
    last = jnp.zeros((16, LANES), F32)
    for j in range(tok.shape[1] // LANES):
        part = jnp.broadcast_to(ids[0:1, j * LANES : (j + 1) * LANES], (16, LANES))
        last = jnp.where(row == j, part, last)
    whole = jnp.concatenate(tiles + [last], axis=0).astype(BF16)
    for sh in range(msg.shape[0]):
        msg[sh] = whole


def split_kernel(where_ref, keep, came, kept, sent, *, xs):
    bit = where_ref[3]
    for i in range(kept.shape[0]):
        high, low = i // xs, i % xs
        one = (high * 2 + bit) * xs + low
        two = (high * 2 + 1 - bit) * xs + low
        kept[i] = (keep[one].astype(F32) + came[one].astype(F32)).astype(BF16)
        sent[i] = (keep[two].astype(F32) + came[two].astype(F32)).astype(BF16)


def sum_kernel(got, sums, msg):
    total = got[0].astype(F32)
    for i in range(1, got.shape[0]):
        total += got[i].astype(F32)
    sums[...] = total
    piece = total[0 : msg.shape[1], :].astype(BF16)
    for i in range(msg.shape[0]):
        msg[i] = piece


def pack_kernel(kept, came, sums, msg):
    groups, rows, dim = kept.shape
    peers, own, _ = msg.shape
    shards = peers // groups
    lane = lax.broadcasted_iota(jnp.int32, (16, LANES), 1)
    row = lax.broadcasted_iota(jnp.int32, (16, LANES), 0)
    small = jnp.where(lane < own + 4, pltpu.roll(sums[...], 10, 0), 0.0)
    small = jnp.where(row < 10, pltpu.roll(small, 96, 1), 0.0)
    small = jnp.concatenate([small, jnp.zeros((own - 16, LANES), F32)], axis=0)
    for g in range(groups):
        block = kept[g].astype(F32) + came[g].astype(F32)
        block = jnp.concatenate([block, jnp.zeros((LANES - rows, dim), F32)], axis=0).T
        for sh in range(shards):
            part = block[sh * own : (sh + 1) * own, :] + small
            msg[g * shards + sh] = part.astype(BF16)


def final_kernel(got, emb, escale, g_mlp, g_emb, g_gin, g_conv, g_mid):
    peers = got.shape[0]
    own, rows = g_mlp.shape
    dim = emb.shape[1]
    shards = dim // own
    lane = lax.broadcasted_iota(jnp.int32, (16, LANES), 1)
    total = jnp.zeros(got.shape[1:], F32)
    acc = jnp.zeros((16, dim), F32)
    head = jnp.zeros((16, LANES), F32)
    for i in range(peers):
        x = got[i].astype(F32)
        total += x
        if i < shards:
            x = x[0:16, :]
            head += x
            y = jnp.where((lane >= 96) & (lane < 96 + own), x, 0.0)
            wide = jnp.concatenate([y, jnp.zeros((16, dim - LANES), F32)], axis=1)
            shift = (i * own - 96) % dim
            acc += wide if shift == 0 else pltpu.roll(wide, shift, 1)
    g_mlp[...] = total[:, 0:rows]
    turned = jnp.concatenate([head, jnp.zeros((LANES - 16, LANES), F32)], axis=0).T
    at = 96 + own
    pull = turned[at : at + 4, 0:1]
    e = escale[...]
    g_emb[...] = acc[0:4, :] - emb[...] * (e * e * e * pull * (1.0 / dim))
    g_gin[...] = acc[4, :]
    g_mid[...] = acc[9, :]
    g_conv[...] = acc[5:9, :]


def filter_kernel(msg, ohq, spec, lf, cols, escale_ref, qt, packed, gf, *, span):
    shards = msg.shape[0]
    _, groups, _, group = ohq.shape
    own_ch = lf.shape[0]
    per_block = shards // groups
    lanes = span // LANES
    parts = [msg[sh].astype(F32) for sh in range(shards)]
    rows = []
    for s in range(2):
        for b in range(groups):
            tiles = []
            for q in range(per_block):
                x = parts[b * per_block + q]
                for h in range(lanes):
                    at = (s * lanes + h) * own_ch
                    tiles.append(x[at : at + own_ch, :])
            rows.append(jnp.concatenate(tiles, axis=1))
    df = jnp.concatenate(rows, axis=0).astype(BF16)
    ds = dot(df, qt[...]).astype(BF16).astype(F32)
    total = jnp.zeros((own_ch, group), F32)
    g = jnp.zeros((own_ch, 16), F32)
    for s in range(2):
        for b in range(groups):
            at = (s * groups + b) * own_ch
            d = ds[at : at + own_ch, :]
            total += d * spec[at : at + own_ch, :].astype(BF16).astype(F32)
            both = dot_nt((lf[...] * d).astype(BF16), ohq[s, b, 16:48, :])
            g += both[:, 0:16] + both[:, 16:32]
    for c in range(group // LANES):
        gf[c * own_ch : (c + 1) * own_ch, :] = total[:, c * LANES : (c + 1) * LANES]
    emb = cols[:, 0:4]
    taps = cols[:, 4:8]
    ntab = cols[:, 8:12]
    gin = cols[:, 12:13]
    escale = escale_ref[...]
    dn = jnp.zeros((own_ch, 4), F32)
    conv = []
    for k in range(4):
        gk = g[:, 4 * k : 4 * k + 4]
        dn += taps[:, k : k + 1] * gk
        conv.append(jnp.sum(ntab * gk, axis=1, keepdims=True))
    at = 2 * lanes * own_ch
    direct = parts[0][at : at + own_ch, :]
    for sh in range(1, shards):
        direct += parts[sh][at : at + own_ch, :]
    demb = escale * gin * dn + direct[:, 0:4]
    dgin = jnp.sum(dn * emb * escale, axis=1, keepdims=True)
    pull = jnp.sum(gin * dn * emb, axis=0, keepdims=True)
    lane = lax.broadcasted_iota(jnp.int32, (own_ch, LANES), 1)
    values = [demb[:, t : t + 1] for t in range(4)] + [dgin] + conv + [direct[:, 4:5]]
    table = jnp.zeros((own_ch, LANES), F32)
    for i, val in enumerate(values):
        table = jnp.where(lane == i, val, table)
    square = jnp.concatenate([table, jnp.zeros((LANES - own_ch, LANES), F32)], axis=0).T
    small = square[0:16, :]
    lane = lax.broadcasted_iota(jnp.int32, (16, LANES), 1)
    row = lax.broadcasted_iota(jnp.int32, (16, LANES), 0)
    for t in range(4):
        value = jnp.broadcast_to(pull[:, t : t + 1], (16, LANES))
        small = jnp.where((row == 0) & (lane == own_ch + t), value, small)
    small = pltpu.roll(small, 6, 0)
    peers = packed.shape[0]
    piece = group // LANES * own_ch // peers
    for i in range(peers):
        at = min(i * piece // 8 * 8, group // LANES * own_ch - 16)
        block = gf[at : at + 16, :]
        off = i * piece - at
        if off:
            block = pltpu.roll(block, 16 - off, 0)
        packed[i] = jnp.where(row < piece, block, small).astype(BF16)


def split_to(x, axis):
    return lax.all_to_all(x, axis, 0, 0, tiled=True)


def swapped(x, axis, distance):
    return lax.ppermute(x, axis, [(i, i ^ distance) for i in range(lax.axis_size(axis))])


def added(a, b):
    return (a.astype(F32) + b.astype(F32)).astype(BF16)


def halved(parts, axis, distance, dim):
    bit = (lax.axis_index(axis) // distance) % 2
    sent = lax.dynamic_index_in_dim(parts, 1 - bit, dim, keepdims=False)
    kept = lax.dynamic_index_in_dim(parts, bit, dim, keepdims=False)
    return kept, swapped(sent, axis, distance)


def kernel_call(body, outs, ins, scratch=(), smem=0, flops=0, name=None):
    vmem = pl.BlockSpec(memory_space=pltpu.VMEM)
    moved = sum(x.size * x.dtype.itemsize for x in ins)
    moved += sum(int(np.prod(o.shape)) * o.dtype.itemsize for o in outs)
    return pl.pallas_call(
        body,
        out_shape=tuple(outs),
        in_specs=[pl.BlockSpec(memory_space=pltpu.SMEM)] * smem + [vmem] * (len(ins) - smem),
        out_specs=tuple([vmem] * len(outs)),
        scratch_shapes=list(scratch),
        compiler_params=pltpu.CompilerParams(vmem_limit_bytes=48 * 1024 * 1024),
        cost_estimate=pl.CostEstimate(flops=flops, bytes_accessed=moved, transcendentals=0),
        name=name,
    )(*ins)


def on_device(tokens, embedding, gain_in, conv_taps, long_filter, gain_mid, mlp_weights, cotangent):
    span = tokens.shape[1]
    dim = embedding.shape[1]
    hidden = mlp_weights.shape[0] // 3
    own_ch, group = long_filter.shape
    shards = lax.axis_size(SEQ)
    dps = lax.axis_size(DP)
    ys, xs = lax.axis_size("dp_y"), lax.axis_size("dp_x")
    chips = 2 * ys * xs
    per_block = group // span
    groups = shards // per_block
    chunks = group // LANES
    half = chunks // 2
    place = lax.axis_index(SEQ)
    core = lax.axis_index("dp_c")
    shape = jax.ShapeDtypeStruct

    vec = jnp.stack([place, core, place // per_block, lax.axis_index("dp_n")])
    where = vec.astype(jnp.int32)
    (msg,) = kernel_call(
        gather_kernel,
        [shape((shards, half * own_ch + 16, LANES), BF16)],
        [where, long_filter, tokens],
        smem=1,
        name="gather",
    )
    gath = split_to(msg, SEQ)

    table = dct_table(group)
    qt = jnp.asarray(np.ascontiguousarray(table.T))
    qown = lax.dynamic_slice_in_dim(jnp.asarray(table), (place % per_block) * span, span, 1)
    emb_t = embedding.T
    escale = lax.rsqrt(jnp.mean(emb_t * emb_t, axis=0, keepdims=True) + 1e-06)
    ntab = (emb_t * escale * gain_in[:, None]).astype(BF16).astype(F32)
    coef = (conv_taps[:, :, None] * ntab[:, None, :]).reshape(dim, 16)
    chigh = coef.astype(BF16)
    clow = (coef - chigh.astype(F32)).astype(BF16)
    acat = jnp.concatenate([chigh, clow, chigh], axis=1)
    cols = jnp.concatenate(
        [emb_t, conv_taps, ntab, gain_in[:, None], gain_mid[:, None], jnp.zeros((dim, 2), F32)], axis=1
    )
    wt = mlp_weights.T
    acat_own = lax.dynamic_slice_in_dim(acat, place * own_ch, own_ch, 0)
    cols_own = lax.dynamic_slice_in_dim(cols, place * own_ch, own_ch, 0)

    bo, ba = kernel_call(
        back_kernel,
        [shape((dim, 2 * span), BF16), shape((hidden, 2 * span), BF16)],
        [cotangent[0], mlp_weights[2 * hidden :]],
        flops=4 * hidden * dim * span,
        name="back",
    )
    gath, bo, ba, wt, qown, acat, cols, acat_own, cols_own = lax.optimization_barrier(
        (gath, bo, ba, wt, qown, acat, cols, acat_own, cols_own)
    )
    gath_other = swapped(gath, "dp_c", 1)
    ohq, spec_own = kernel_call(
        partial(dct_kernel, half_rows=half * own_ch, per_block=per_block),
        [shape((2, groups, 48, group), BF16), shape((2 * groups * own_ch, group), F32)],
        [gath, acat_own, qt],
        flops=2 * 128 * group * group,
        name="bases",
    )
    lanes = 2 * span // LANES
    msg_rows = (lanes + 1) * own_ch
    msg_rows += -msg_rows % 16
    own_rows = 3 * hidden // dps
    df_msg, act, level, keep, send = kernel_call(
        mid_kernel,
        [
            shape((shards, msg_rows, LANES), BF16),
            shape((hidden, 2 * span), BF16),
            shape((dim, 2 * span), F32),
            shape((chips, own_rows, dim), BF16),
            shape((chips, own_rows, dim), BF16),
        ],
        [where, gath, gath_other, tokens, cols, acat, mlp_weights, wt, qown, ohq, bo, ba],
        scratch=[
            pltpu.VMEM((chunks, dim, LANES), F32),
            pltpu.VMEM((dim, group), BF16),
            pltpu.VMEM((dim, 2 * span), F32),
            pltpu.VMEM((dim, 2 * span), BF16),
            pltpu.VMEM((2 * hidden, 2 * span), BF16),
            pltpu.VMEM((3 * hidden, dim), F32),
        ],
        smem=1,
        flops=12 * hidden * dim * span,
        name="mid",
    )
    df_parts = split_to(df_msg, SEQ)
    (layer,) = kernel_call(
        out_kernel, [shape((2 * dim, span), BF16)], [level, act, wt], flops=4 * hidden * dim * span, name="out"
    )
    came, df_parts = lax.optimization_barrier((swapped(send, "dp_c", 1), df_parts))
    kept, sent = kernel_call(
        partial(split_kernel, xs=xs),
        [shape((chips // 2, own_rows, dim), BF16)] * 2,
        [where, keep, came],
        smem=1,
        name="split",
    )
    block = added(kept, swapped(sent, "dp_n", 1)).reshape(ys, xs, own_rows, dim)
    kept, came = halved(block, "dp_x", 1, 1)

    piece = chunks * own_ch // dps
    (packed,) = kernel_call(
        partial(filter_kernel, span=span),
        [shape((dps, 16, LANES), BF16)],
        [df_parts, ohq, spec_own, long_filter, cols_own, escale, qt],
        scratch=[pltpu.VMEM((chunks * own_ch, LANES), F32)],
        flops=4 * groups * own_ch * group * group,
        name="filter",
    )
    summed, pieces = kernel_call(
        sum_kernel,
        [shape((16, LANES), F32), shape((dps, piece, LANES), BF16)],
        [split_to(packed, DP)],
        name="sum",
    )
    whole = split_to(pieces, DP)
    grad_filter = (
        jnp.swapaxes(whole.astype(F32).reshape(chunks, own_ch, LANES), 0, 1).reshape(own_ch, group)
    )
    cols_each = dim // shards
    (final,) = kernel_call(
        pack_kernel, [shape((ys * shards, own_ch, LANES), BF16)], [kept, came, summed], name="pack"
    )
    final = split_to(final, LAST)
    grad_mlp, grad_embedding, grad_gain_in, grad_conv, grad_gain_mid = kernel_call(
        final_kernel,
        [
            shape((cols_each, own_rows), F32),
            shape((4, dim), F32),
            shape((dim,), F32),
            shape((4, dim), F32),
            shape((dim,), F32),
        ],
        [final, embedding, escale.reshape(4, 1)],
        name="final",
    )
    grad_mlp, grad_conv = grad_mlp.T, grad_conv.T
    return layer[None], grad_embedding, grad_gain_in, grad_conv, grad_filter, grad_gain_mid, grad_mlp


def solution(mesh):
    dps, seqs = mesh.devices.shape
    torus = Mesh(mesh.devices.reshape(dps // 8, 2, 2, 2, seqs // 2, 2), DP + SEQ)
    return jax.shard_map(
        on_device,
        mesh=torus,
        in_specs=(P(DP, SEQ), P(), P(), P(), P(SEQ, None), P(), P(), P(DP, None, SEQ)),
        out_specs=(P(DP, None, SEQ), P(), P(), P(), P(SEQ, None), P(), P(DP, SEQ)),
        check_vma=False,
    )
```

```python
from functools import partial

import jax
import jax.numpy as jnp
import numpy as np
from jax import lax
from jax.experimental import pallas as pl
from jax.experimental.pallas import tpu as pltpu
from jax.sharding import Mesh
from jax.sharding import PartitionSpec as P

DP = ("dp_y", "dp_x", "dp_c")
CHIPS = ("dp_y", "dp_x")
SEQ = ("seq_z", "seq_x")
F32, BF16 = jnp.float32, jnp.bfloat16
LANES = 128


def dct_table(length):
    freq = np.arange(length, dtype=np.int64)[:, None]
    place = np.arange(length, dtype=np.int64)[None, :]
    phase = (2 * place + 1) * freq % (4 * length)
    weight = np.where(freq == 0, np.sqrt(1.0 / length), np.sqrt(2.0 / length))
    return (weight * np.cos(np.pi * phase / (2 * length))).astype(np.float32).astype(jnp.bfloat16)


def dot(a, b):
    return jnp.dot(a, b, preferred_element_type=F32)


def dot_nt(a, b):
    return lax.dot_general(a, b, (((1,), (1,)), ((), ())), preferred_element_type=F32)


def onehot_rows(gath, groups, group, half_rows, per_block):
    shards = gath.shape[0]
    rows_of = 2
    ids = [gath[sh, half_rows : half_rows + 16, :].astype(F32) for sh in range(shards)]
    rows = [ids[sh][j : j + 1, :] for sh in range(shards) for j in range(rows_of)]
    outside = jnp.full((1, LANES), -1.0, F32)
    rows = [outside] + rows + [outside]
    per = per_block * rows_of
    width = group + 2 * LANES
    row = lax.broadcasted_iota(jnp.int32, (32, group), 0)
    want = jnp.where(row < 16, row % 4, 3 - row % 4).astype(F32)
    onehots = []
    for b in range(groups):
        pieces = rows[b * per : b * per + per + 2]
        ext = jnp.concatenate([jnp.broadcast_to(p, (8, LANES)) for p in pieces], axis=1)
        picked = jnp.zeros((32, group), F32)
        for j in range(8):
            shift = j if j < 4 else (width - (j - 4)) % width
            moved = ext if shift == 0 else pltpu.roll(ext, shift, 1)
            moved = jnp.broadcast_to(moved[0:1, LANES : LANES + group], (32, group))
            picked = jnp.where(row // 4 == j, moved, picked)
        onehots.append(jnp.where(picked == want, 1.0, 0.0).astype(BF16))
    return onehots


def dct_kernel(gath, qt, ohq, *, half_rows, per_block):
    _, groups, _, group = ohq.shape
    onehots = onehot_rows(gath, groups, group, half_rows, per_block)
    both = dot(jnp.concatenate(onehots, axis=0), qt[...])
    for b in range(groups):
        x = both[32 * b : 32 * b + 32, :]
        high = x.astype(BF16)
        low = (x - high.astype(F32)).astype(BF16)
        for s in range(2):
            o_high = high[16 * s : 16 * s + 16]
            o_low = low[16 * s : 16 * s + 16]
            ocat = jnp.concatenate([o_high, o_high, o_low], axis=0)
            ohq[s, b] = ocat


def back_kernel(cot, w, bo, ba):
    dim, span = cot.shape[0] // 2, cot.shape[1]
    ri = lax.broadcasted_iota(jnp.int32, (dim, dim), 0)
    ci = lax.broadcasted_iota(jnp.int32, (dim, dim), 1)
    turn = jnp.where(ri + ci == dim - 1, 1.0, 0.0).astype(BF16)
    bo[:, 0:span] = cot[0:dim, :]
    bo[:, span : 2 * span] = dot(turn, cot[dim : 2 * dim, :]).astype(BF16)
    hidden = ba.shape[0]
    for r in range(0, hidden, 256):
        ba[r : r + 256, :] = dot(w[2 * hidden + r : 2 * hidden + r + 256, :], bo[...]).astype(BF16)


def mid_kernel(
    where_ref, ga, gb, tok_ref, cols, acat, w, wt, qown, qtown, ohq, bo, ba,
    act_s, level_s, keep, send,
    lf_s, scaled_s, spec_s, df_s, m_s, bproj_s, acc_s, gf_s, tail_s,
):
    shards = ga.shape[0]
    chunks, dim, _ = lf_s.shape
    own_ch = dim // shards
    hidden = act_s.shape[0]
    span = tok_ref.shape[1]
    half = chunks // 2
    body_rows = half * own_ch
    core = where_ref[1]
    block = where_ref[2]
    chips, out_rows, _ = keep.shape
    rows = (3 * hidden) // (2 * chips)
    freqs = chunks * LANES // (2 * chips)
    for sh in range(shards):
        for c in range(half):
            src = slice(c * own_ch, (c + 1) * own_ch)
            dst = slice(sh * own_ch, (sh + 1) * own_ch)
            lf_s[core * half + c, dst, :] = ga[sh, 0:body_rows, :].astype(F32)[src, :]
            lf_s[(1 - core) * half + c, dst, :] = gb[sh, 0:body_rows, :].astype(F32)[src, :]
    emb = cols[:, 0:4]
    gmid = cols[:, 13:14]
    tok = tok_ref[...].astype(F32)
    step = 128
    gmid_part = jnp.zeros((dim, 1), F32)
    direct = jnp.zeros((dim, 16), F32)
    taps_part = [jnp.zeros((step, 16), F32) for _ in range(dim // step)]
    for s in range(2):
        here = slice(s * span, (s + 1) * span)
        ocat = ohq[s, block]
        for r in range(0, dim, step):
            spec = dot(acat[r : r + step, :], ocat).astype(BF16)
            spec_s[r : r + step, :] = spec
            spec = spec.astype(F32)
            for c in range(chunks):
                lanes = slice(c * LANES, (c + 1) * LANES)
                scaled_s[r : r + step, lanes] = (lf_s[c, r : r + step, :] * spec[:, lanes]).astype(BF16)
        filt = dot(scaled_s[...], qown[...]).astype(BF16).astype(F32)
        ids = tok if s == 0 else 3.0 - tok
        resid = jnp.broadcast_to(emb[:, 3:4], (dim, span))
        for t in range(3):
            resid = jnp.where(ids == float(t), emb[:, t : t + 1], resid)
        level = resid + filt
        level_s[:, here] = level
        scale = lax.rsqrt(jnp.sum(level * level, axis=0, keepdims=True) * (1.0 / dim) + 1e-06)
        m_s[:, here] = (level * scale * gmid).astype(BF16)
        normed = m_s[:, here]
        part = 256
        for h in range(0, hidden, part):
            gate = dot(w[h : h + part, :], normed).astype(BF16).astype(F32)
            up = dot(w[hidden + h : hidden + h + part, :], normed).astype(BF16).astype(F32)
            b = ba[h : h + part, here].astype(F32)
            sig = jax.nn.sigmoid(gate)
            swish = gate * sig
            act_s[h : h + part, here] = (swish * up).astype(BF16)
            bproj_s[h : h + part, here] = (b * up * sig * (1.0 + gate * (1.0 - sig))).astype(BF16)
            bproj_s[hidden + h : hidden + h + part, here] = (b * swish).astype(BF16)
        bmid = dot(wt[:, 0 : 2 * hidden], bproj_s[:, here]).astype(BF16).astype(F32)
        level = level_s[:, here]
        gmid_part += jnp.sum(bmid * level * scale, axis=1, keepdims=True)
        weighed = bmid * gmid
        pull = jnp.sum(weighed * level, axis=0, keepdims=True)
        dlevel = (
            bo[:, here].astype(F32)
            + scale * weighed
            - level * (scale * scale * scale * pull * (1.0 / dim))
        )
        dfilt = dlevel.astype(BF16)
        df_s[...] = dfilt
        base = lax.broadcasted_iota(jnp.int32, (16, span), 0).astype(F32)
        mine = jnp.where(ids == base, 1.0, 0.0).astype(BF16)
        direct += dot_nt(dfilt, mine)
        for i, r in enumerate(range(0, dim, step)):
            ds = dot(df_s[r : r + step, :], qtown[...])
            term = ds * spec_s[r : r + step, :].astype(F32)
            if s == 0:
                gf_s[r : r + step, :] = term
            else:
                gf_s[r : r + step, :] += term
            for c in range(chunks):
                lanes = slice(c * LANES, (c + 1) * LANES)
                scaled_s[r : r + step, lanes] = (lf_s[c, r : r + step, :] * ds[:, lanes]).astype(BF16)
            both = dot_nt(scaled_s[r : r + step, :], ocat[16:48, :])
            taps_part[i] += both[:, 0:16] + both[:, 16:32]
    taps = cols[:, 4:8]
    ntab = cols[:, 8:12]
    gin = cols[:, 12:13]
    g = jnp.concatenate(taps_part, axis=0)
    dn = jnp.zeros((dim, 4), F32)
    conv = []
    for k in range(4):
        gk = g[:, 4 * k : 4 * k + 4]
        dn += taps[:, k : k + 1] * gk
        conv.append(jnp.sum(ntab * gk, axis=1, keepdims=True))
    escale = lax.rsqrt(jnp.sum(emb * emb, axis=0, keepdims=True) * (1.0 / dim) + 1e-06)
    epull = jnp.sum(gin * dn * emb, axis=0, keepdims=True)
    demb = escale * gin * dn - emb * (escale * escale * escale * epull * (1.0 / dim))
    demb += direct[:, 0:4]
    dgin = jnp.sum(dn * emb * escale, axis=1, keepdims=True)
    lane = lax.broadcasted_iota(jnp.int32, (dim, LANES), 1)
    small = jnp.zeros((dim, LANES), F32)
    values = [demb[:, t : t + 1] for t in range(4)] + [dgin] + conv + [gmid_part]
    for i, val in enumerate(values):
        small = jnp.where(lane == i, val, small)
    small = small.T
    filler = out_rows - rows - freqs
    base = lax.broadcasted_iota(jnp.int32, (filler, dim), 0)
    for c in range(chunks):
        turned = gf_s[:, c * LANES : (c + 1) * LANES].T
        for q in range(LANES // freqs):
            k = c * (LANES // freqs) + q
            tail = jnp.zeros((filler, dim), F32)
            if k < len(values):
                tail = jnp.where(base == 0, small[k : k + 1, :], 0.0)
            tail_s[k] = jnp.concatenate([turned[q * freqs : (q + 1) * freqs, :], tail], axis=0)
    part = hidden
    for r in range(0, 2 * hidden, part):
        acc_s[r : r + part, :] = dot_nt(bproj_s[r : r + part, :], m_s[...])
    acc_s[2 * hidden : 3 * hidden, :] = dot_nt(act_s[...], bo[...])
    for i in range(chips):
        for dst, k in ((keep, 2 * i + core), (send, 2 * i + 1 - core)):
            weights = acc_s[pl.ds(pl.multiple_of(k * rows, 8), rows), :]
            dst[i] = jnp.concatenate([weights, tail_s[k]], axis=0).astype(BF16)


def out_kernel(level, act, wt, out):
    dim, span = level.shape[0], level.shape[1] // 2
    hidden = act.shape[0]
    ri = lax.broadcasted_iota(jnp.int32, (dim, dim), 0)
    ci = lax.broadcasted_iota(jnp.int32, (dim, dim), 1)
    turn = jnp.where(ri + ci == dim - 1, 1.0, 0.0).astype(BF16)
    z = level[...] + dot(wt[:, 2 * hidden : 3 * hidden], act[...])
    z = z.astype(BF16)
    out[0:dim, :] = z[:, 0:span]
    out[dim : 2 * dim, :] = dot(turn, z[:, span : 2 * span]).astype(BF16)


def gather_kernel(where_ref, lf, tok, msg):
    own_ch, group = lf.shape
    half = group // LANES // 2
    core = where_ref[1]
    tiles = []
    for c in range(half):
        at = pl.multiple_of((core * half + c) * LANES, LANES)
        tiles.append(lf[:, pl.ds(at, LANES)])
    ids = jnp.broadcast_to(tok[...].astype(F32), (8, tok.shape[1]))
    row = lax.broadcasted_iota(jnp.int32, (16, LANES), 0)
    last = jnp.zeros((16, LANES), F32)
    for j in range(tok.shape[1] // LANES):
        part = jnp.broadcast_to(ids[0:1, j * LANES : (j + 1) * LANES], (16, LANES))
        last = jnp.where(row == j, part, last)
    whole = jnp.concatenate(tiles + [last], axis=0).astype(BF16)
    for sh in range(msg.shape[0]):
        msg[sh] = whole


def prep_kernel(emb, taps, gin, gmid, cols, acat):
    dim = emb.shape[1]
    e = emb[...]
    scale = lax.rsqrt(jnp.sum(e * e, axis=1, keepdims=True) * (1.0 / dim) + 1e-06)
    ntab = (e * scale * gin[...]).astype(BF16).astype(F32)
    rows = [e[t : t + 1, :] for t in range(4)] + [taps[k : k + 1, :] for k in range(4)]
    rows += [ntab[t : t + 1, :] for t in range(4)] + [gin[...], gmid[...]]
    row = lax.broadcasted_iota(jnp.int32, (LANES, dim), 0)
    table = jnp.zeros((LANES, dim), F32)
    for i, r in enumerate(rows):
        table = jnp.where(row == i, r, table)
    cols[...] = table.T
    coefs = jnp.zeros((LANES, dim), F32)
    for k in range(4):
        for t in range(4):
            value = taps[k : k + 1, :] * ntab[t : t + 1, :]
            high = value.astype(BF16).astype(F32)
            at = 4 * k + t
            coefs = jnp.where((row == at) | (row == 32 + at), high, coefs)
            coefs = jnp.where(row == 16 + at, value - high, coefs)
    acat[...] = coefs.T[:, 0:48].astype(BF16)


def over_chips_kernel(got, msg, *, rows, freqs):
    total = got[0].astype(F32)
    for i in range(1, got.shape[0]):
        total += got[i].astype(F32)
    dim = total.shape[1]
    own = dim // msg.shape[0]
    kept = total[0 : rows + freqs, :]
    turned = jnp.concatenate([kept, jnp.zeros((LANES - rows - freqs, dim), F32)], axis=0).T
    small = total[rows + freqs : rows + freqs + 1, :]
    row = lax.broadcasted_iota(jnp.int32, (8, LANES), 0)
    lines = jnp.zeros((8, LANES), F32)
    for j in range(dim // LANES):
        lines = jnp.where(row == j, small[:, j * LANES : (j + 1) * LANES], lines)
    for sh in range(msg.shape[0]):
        part = turned[sh * own : (sh + 1) * own, :]
        msg[sh] = jnp.concatenate([part, lines], axis=0).astype(BF16)


def over_seq_kernel(got, g_mlp, msg, *, freqs):
    total = got[0].astype(F32)
    for i in range(1, got.shape[0]):
        total += got[i].astype(F32)
    own, rows = g_mlp.shape
    g_mlp[...] = total[0:own, 0:rows]
    lane = lax.broadcasted_iota(jnp.int32, (own, LANES), 1)
    part = jnp.where(lane < freqs, pltpu.roll(total[0:own, :], LANES - rows, 1), 0.0)
    first = part[0:8, :]
    for j in range(1, own // 8):
        first += pltpu.roll(part[8 * j : 8 * j + 8, :], freqs * j, 1)
    whole = jnp.concatenate([first, total[own : own + 8, :]], axis=0).astype(BF16)
    for i in range(msg.shape[0]):
        msg[i] = whole


def final_kernel(got, g_filter, g_emb, g_gin, g_conv, g_mid):
    own, group = g_filter.shape
    dim = g_emb.shape[1]
    peers = got.shape[0]
    freqs = group // peers
    per = LANES // freqs
    lane = lax.broadcasted_iota(jnp.int32, (8, LANES), 1)
    lines = []
    for c in range(group // LANES):
        tiles = [jnp.zeros((8, LANES), F32) for _ in range(own // 8)]
        for q in range(per):
            x = got[c * per + q].astype(F32)
            if len(lines) < 10:
                lines.append([x[8 + j : 9 + j, :] for j in range(dim // LANES)])
            mine = (lane >= q * freqs) & (lane < (q + 1) * freqs)
            for j in range(own // 8):
                shift = (q - j) * freqs % LANES
                y = x[0:8, :] if shift == 0 else pltpu.roll(x[0:8, :], shift, 1)
                tiles[j] = jnp.where(mine, y, tiles[j])
        for j in range(own // 8):
            g_filter[8 * j : 8 * j + 8, c * LANES : (c + 1) * LANES] = tiles[j]
    for j in range(dim // LANES):
        lanes = slice(j * LANES, (j + 1) * LANES)
        for t in range(4):
            g_emb[t : t + 1, lanes] = lines[t][j]
            g_conv[t : t + 1, lanes] = lines[5 + t][j]
        g_gin[0:1, lanes] = lines[4][j]
        g_mid[0:1, lanes] = lines[9][j]


def split_to(x, axis):
    return lax.all_to_all(x, axis, 0, 0, tiled=True)


def swapped(x, axis, distance):
    return lax.ppermute(x, axis, [(i, i ^ distance) for i in range(lax.axis_size(axis))])


def added(a, b):
    return (a.astype(F32) + b.astype(F32)).astype(BF16)


def kernel_call(body, outs, ins, scratch=(), smem=0, flops=0, name=None):
    vmem = pl.BlockSpec(memory_space=pltpu.VMEM)
    moved = sum(x.size * x.dtype.itemsize for x in ins)
    moved += sum(int(np.prod(o.shape)) * o.dtype.itemsize for o in outs)
    return pl.pallas_call(
        body,
        out_shape=tuple(outs),
        in_specs=[pl.BlockSpec(memory_space=pltpu.SMEM)] * smem + [vmem] * (len(ins) - smem),
        out_specs=tuple([vmem] * len(outs)),
        scratch_shapes=list(scratch),
        compiler_params=pltpu.CompilerParams(vmem_limit_bytes=48 * 1024 * 1024),
        cost_estimate=pl.CostEstimate(flops=flops, bytes_accessed=moved, transcendentals=0),
        name=name,
    )(*ins)


def on_device(tokens, embedding, gain_in, conv_taps, long_filter, gain_mid, mlp_weights, cotangent):
    span = tokens.shape[1]
    dim = embedding.shape[1]
    hidden = mlp_weights.shape[0] // 3
    own_ch, group = long_filter.shape
    shards = lax.axis_size(SEQ)
    dps = lax.axis_size(DP)
    chips = lax.axis_size(CHIPS)
    per_block = group // span
    groups = shards // per_block
    chunks = group // LANES
    half = chunks // 2
    place = lax.axis_index(SEQ)
    core = lax.axis_index("dp_c")
    shape = jax.ShapeDtypeStruct

    vec = jnp.stack([place, core, place // per_block])
    where = vec.astype(jnp.int32)
    (msg,) = kernel_call(
        gather_kernel,
        [shape((shards, half * own_ch + 16, LANES), BF16)],
        [where, long_filter, tokens],
        smem=1,
        name="gather",
    )
    gath = split_to(msg, SEQ)

    table = dct_table(group)
    qt = jnp.asarray(np.ascontiguousarray(table.T))
    inner = (place % per_block) * span
    qown = lax.dynamic_slice_in_dim(jnp.asarray(table), inner, span, 1)
    qtown = lax.dynamic_slice_in_dim(qt, inner, span, 0)
    wt = mlp_weights.T
    cols, acat = kernel_call(
        prep_kernel,
        [shape((dim, LANES), F32), shape((dim, 48), BF16)],
        [embedding, conv_taps.T, gain_in[None], gain_mid[None]],
        name="prep",
    )

    bo, ba = kernel_call(
        back_kernel,
        [shape((dim, 2 * span), BF16), shape((hidden, 2 * span), BF16)],
        [cotangent[0], mlp_weights],
        flops=4 * hidden * dim * span,
        name="back",
    )
    gath, bo, ba, wt, qown, qtown, acat, cols = lax.optimization_barrier(
        (gath, bo, ba, wt, qown, qtown, acat, cols)
    )
    gath_other = swapped(gath, "dp_c", 1)
    (ohq,) = kernel_call(
        partial(dct_kernel, half_rows=half * own_ch, per_block=per_block),
        [shape((2, groups, 48, group), BF16)],
        [gath, qt],
        flops=2 * 128 * group * group,
        name="bases",
    )
    own_rows = 3 * hidden // dps
    freqs = group // dps
    all_rows = own_rows + freqs + 8
    all_rows += -all_rows % 16
    act, level, keep, send = kernel_call(
        mid_kernel,
        [
            shape((hidden, 2 * span), BF16),
            shape((dim, 2 * span), F32),
            shape((chips, all_rows, dim), BF16),
            shape((chips, all_rows, dim), BF16),
        ],
        [where, gath, gath_other, tokens, cols, acat, mlp_weights, wt, qown, qtown, ohq, bo, ba],
        scratch=[
            pltpu.VMEM((chunks, dim, LANES), F32),
            pltpu.VMEM((dim, group), BF16),
            pltpu.VMEM((dim, group), BF16),
            pltpu.VMEM((dim, span), BF16),
            pltpu.VMEM((dim, 2 * span), BF16),
            pltpu.VMEM((2 * hidden, 2 * span), BF16),
            pltpu.VMEM((3 * hidden, dim), F32),
            pltpu.VMEM((dim, group), F32),
            pltpu.VMEM((dps, all_rows - own_rows, dim), F32),
        ],
        smem=1,
        flops=28 * hidden * dim * span,
        name="mid",
    )
    (layer,) = kernel_call(
        out_kernel, [shape((2 * dim, span), BF16)], [level, act, wt], flops=4 * hidden * dim * span, name="out"
    )
    block = split_to(added(keep, swapped(send, "dp_c", 1)), CHIPS)
    (msg,) = kernel_call(
        partial(over_chips_kernel, rows=own_rows, freqs=freqs),
        [shape((shards, own_ch + 8, LANES), BF16)],
        [block],
        name="over_chips",
    )
    grad_mlp, msg = kernel_call(
        partial(over_seq_kernel, freqs=freqs),
        [shape((own_ch, own_rows), F32), shape((dps, 16, LANES), BF16)],
        [split_to(msg, SEQ)],
        name="over_seq",
    )
    grad_filter, grad_embedding, grad_gain_in, grad_conv, grad_gain_mid = kernel_call(
        final_kernel,
        [
            shape((own_ch, group), F32),
            shape((4, dim), F32),
            shape((1, dim), F32),
            shape((4, dim), F32),
            shape((1, dim), F32),
        ],
        [split_to(msg, DP)],
        name="final",
    )
    return (
        layer[None],
        grad_embedding,
        grad_gain_in[0],
        grad_conv.T,
        grad_filter,
        grad_gain_mid[0],
        grad_mlp.T,
    )


def solution(mesh):
    dps, seqs = mesh.devices.shape
    torus = Mesh(mesh.devices.reshape(dps // 4, 2, 2, seqs // 2, 2), DP + SEQ)
    return jax.shard_map(
        on_device,
        mesh=torus,
        in_specs=(P(DP, SEQ), P(), P(), P(), P(SEQ, None), P(), P(), P(DP, None, SEQ)),
        out_specs=(P(DP, None, SEQ), P(), P(), P(), P(SEQ, None), P(), P(DP, SEQ)),
        check_vma=False,
    )
```

```python
from functools import partial

import jax
import jax.numpy as jnp
import numpy as np
from jax import lax
from jax.experimental import pallas as pl
from jax.experimental.pallas import tpu as pltpu
from jax.sharding import Mesh
from jax.sharding import PartitionSpec as P

DP = ("dp_y", "dp_n", "dp_x", "dp_c")
SEQ = ("seq_z", "seq_n", "seq_x")
NEAR = ("dp_n", "dp_x", "seq_n")
FAR = ("dp_y", "seq_z", "seq_x")
F32, BF16 = jnp.float32, jnp.bfloat16
LANES = 128


def dct_table(length):
    freq = np.arange(length, dtype=np.int64)[:, None]
    place = np.arange(length, dtype=np.int64)[None, :]
    phase = (2 * place + 1) * freq % (4 * length)
    weight = np.where(freq == 0, np.sqrt(1.0 / length), np.sqrt(2.0 / length))
    return (weight * np.cos(np.pi * phase / (2 * length))).astype(np.float32).astype(jnp.bfloat16)


def dot(a, b):
    return jnp.dot(a, b, preferred_element_type=F32)


def dot_nt(a, b):
    return lax.dot_general(a, b, (((1,), (1,)), ((), ())), preferred_element_type=F32)


def onehot_rows(gath, groups, group, half_rows, per_block):
    shards = gath.shape[0]
    rows_of = 2
    ids = [gath[sh, half_rows : half_rows + 16, :].astype(F32) for sh in range(shards)]
    rows = [ids[sh][j : j + 1, :] for sh in range(shards) for j in range(rows_of)]
    outside = jnp.full((1, LANES), -1.0, F32)
    rows = [outside] + rows + [outside]
    per = per_block * rows_of
    width = group + 2 * LANES
    row = lax.broadcasted_iota(jnp.int32, (32, group), 0)
    want = jnp.where(row < 16, row % 4, 3 - row % 4).astype(F32)
    onehots = []
    for b in range(groups):
        pieces = rows[b * per : b * per + per + 2]
        ext = jnp.concatenate([jnp.broadcast_to(p, (8, LANES)) for p in pieces], axis=1)
        picked = jnp.zeros((32, group), F32)
        for j in range(8):
            shift = j if j < 4 else (width - (j - 4)) % width
            moved = ext if shift == 0 else pltpu.roll(ext, shift, 1)
            moved = jnp.broadcast_to(moved[0:1, LANES : LANES + group], (32, group))
            picked = jnp.where(row // 4 == j, moved, picked)
        onehots.append(jnp.where(picked == want, 1.0, 0.0).astype(BF16))
    return onehots


def dct_kernel(gath, qt, ohq, *, half_rows, per_block):
    _, groups, _, group = ohq.shape
    onehots = onehot_rows(gath, groups, group, half_rows, per_block)
    both = dot(jnp.concatenate(onehots, axis=0), qt[...])
    for b in range(groups):
        x = both[32 * b : 32 * b + 32, :]
        high = x.astype(BF16)
        low = (x - high.astype(F32)).astype(BF16)
        for s in range(2):
            o_high = high[16 * s : 16 * s + 16]
            o_low = low[16 * s : 16 * s + 16]
            ocat = jnp.concatenate([o_high, o_high, o_low], axis=0)
            ohq[s, b] = ocat


def back_kernel(cot, w, bo, ba):
    dim, span = cot.shape[0] // 2, cot.shape[1]
    ri = lax.broadcasted_iota(jnp.int32, (dim, dim), 0)
    ci = lax.broadcasted_iota(jnp.int32, (dim, dim), 1)
    turn = jnp.where(ri + ci == dim - 1, 1.0, 0.0).astype(BF16)
    bo[:, 0:span] = cot[0:dim, :]
    bo[:, span : 2 * span] = dot(turn, cot[dim : 2 * dim, :]).astype(BF16)
    hidden = ba.shape[0]
    for r in range(0, hidden, 256):
        ba[r : r + 256, :] = dot(w[2 * hidden + r : 2 * hidden + r + 256, :], bo[...]).astype(BF16)


def mid_kernel(
    where_ref, ga, gb, tok_ref, cols, acat, w, wt, qown, qtown, ohq, bo, ba,
    act_s, level_s, keep, send,
    lf_s, scaled_s, spec_s, df_s, m_s, bproj_s, acc_s, gf_s, tail_s,
):
    shards = ga.shape[0]
    chunks, dim, _ = lf_s.shape
    own_ch = dim // shards
    hidden = act_s.shape[0]
    span = tok_ref.shape[1]
    half = chunks // 2
    body_rows = half * own_ch
    core = where_ref[1]
    block = where_ref[2]
    near, far, out_rows, _ = keep.shape
    chips = near // 2 * far
    rows = (3 * hidden) // (2 * chips)
    freqs = chunks * LANES // (2 * chips)
    pair = 2 * own_ch
    order = list(range(0, shards // 2, 2)) + list(range(1, shards // 2, 2))

    def ordered(ref, lanes):
        return jnp.concatenate([ref[g * pair : (g + 1) * pair, lanes] for g in order], axis=0)

    for sh in range(shards):
        for c in range(half):
            src = slice(c * own_ch, (c + 1) * own_ch)
            dst = slice(sh * own_ch, (sh + 1) * own_ch)
            lf_s[core * half + c, dst, :] = ga[sh, 0:body_rows, :].astype(F32)[src, :]
            lf_s[(1 - core) * half + c, dst, :] = gb[sh, 0:body_rows, :].astype(F32)[src, :]
    emb = cols[:, 0:4]
    gmid = cols[:, 13:14]
    tok = tok_ref[...].astype(F32)
    step = 128
    gmid_part = jnp.zeros((dim, 1), F32)
    direct = jnp.zeros((dim, 16), F32)
    taps_part = [jnp.zeros((step, 16), F32) for _ in range(dim // step)]
    for s in range(2):
        here = slice(s * span, (s + 1) * span)
        ocat = ohq[s, block]
        for r in range(0, dim, step):
            spec = dot(acat[r : r + step, :], ocat).astype(BF16)
            spec_s[r : r + step, :] = spec
            spec = spec.astype(F32)
            for c in range(chunks):
                lanes = slice(c * LANES, (c + 1) * LANES)
                scaled_s[r : r + step, lanes] = (lf_s[c, r : r + step, :] * spec[:, lanes]).astype(BF16)
        filt = dot(scaled_s[...], qown[...]).astype(BF16).astype(F32)
        ids = tok if s == 0 else 3.0 - tok
        resid = jnp.broadcast_to(emb[:, 3:4], (dim, span))
        for t in range(3):
            resid = jnp.where(ids == float(t), emb[:, t : t + 1], resid)
        level = resid + filt
        level_s[:, here] = level
        scale = lax.rsqrt(jnp.sum(level * level, axis=0, keepdims=True) * (1.0 / dim) + 1e-06)
        m_s[:, here] = (level * scale * gmid).astype(BF16)
        normed = m_s[:, here]
        part = 256
        for h in range(0, hidden, part):
            gate = dot(w[h : h + part, :], normed).astype(BF16).astype(F32)
            up = dot(w[hidden + h : hidden + h + part, :], normed).astype(BF16).astype(F32)
            b = ba[h : h + part, here].astype(F32)
            sig = jax.nn.sigmoid(gate)
            swish = gate * sig
            act_s[h : h + part, here] = (swish * up).astype(BF16)
            bproj_s[h : h + part, here] = (b * up * sig * (1.0 + gate * (1.0 - sig))).astype(BF16)
            bproj_s[hidden + h : hidden + h + part, here] = (b * swish).astype(BF16)
        bmid = dot(wt[:, 0 : 2 * hidden], bproj_s[:, here]).astype(BF16).astype(F32)
        level = level_s[:, here]
        gmid_part += jnp.sum(bmid * level * scale, axis=1, keepdims=True)
        weighed = bmid * gmid
        pull = jnp.sum(weighed * level, axis=0, keepdims=True)
        dlevel = (
            bo[:, here].astype(F32)
            + scale * weighed
            - level * (scale * scale * scale * pull * (1.0 / dim))
        )
        dfilt = dlevel.astype(BF16)
        df_s[...] = dfilt
        base = lax.broadcasted_iota(jnp.int32, (16, span), 0).astype(F32)
        mine = jnp.where(ids == base, 1.0, 0.0).astype(BF16)
        direct += dot_nt(dfilt, mine)
        for i, r in enumerate(range(0, dim, step)):
            ds = dot(df_s[r : r + step, :], qtown[...])
            term = ds * spec_s[r : r + step, :].astype(F32)
            if s == 0:
                gf_s[r : r + step, :] = term
            else:
                gf_s[r : r + step, :] += term
            for c in range(chunks):
                lanes = slice(c * LANES, (c + 1) * LANES)
                scaled_s[r : r + step, lanes] = (lf_s[c, r : r + step, :] * ds[:, lanes]).astype(BF16)
            both = dot_nt(scaled_s[r : r + step, :], ocat[16:48, :])
            taps_part[i] += both[:, 0:16] + both[:, 16:32]
    taps = cols[:, 4:8]
    ntab = cols[:, 8:12]
    gin = cols[:, 12:13]
    g = jnp.concatenate(taps_part, axis=0)
    dn = jnp.zeros((dim, 4), F32)
    conv = []
    for k in range(4):
        gk = g[:, 4 * k : 4 * k + 4]
        dn += taps[:, k : k + 1] * gk
        conv.append(jnp.sum(ntab * gk, axis=1, keepdims=True))
    escale = lax.rsqrt(jnp.sum(emb * emb, axis=0, keepdims=True) * (1.0 / dim) + 1e-06)
    epull = jnp.sum(gin * dn * emb, axis=0, keepdims=True)
    demb = escale * gin * dn - emb * (escale * escale * escale * epull * (1.0 / dim))
    demb += direct[:, 0:4]
    dgin = jnp.sum(dn * emb * escale, axis=1, keepdims=True)
    lane = lax.broadcasted_iota(jnp.int32, (dim, LANES), 1)
    small = jnp.zeros((dim, LANES), F32)
    values = [demb[:, t : t + 1] for t in range(4)] + [dgin] + conv + [gmid_part]
    for i, val in enumerate(values):
        small = jnp.where(lane == i, val, small)
    small = small.T
    filler = 2 * out_rows - rows - freqs
    base = lax.broadcasted_iota(jnp.int32, (filler, dim), 0)
    left = lax.broadcasted_iota(jnp.int32, (filler, dim), 1) < dim // 2
    for c in range(chunks):
        turned = ordered(gf_s, slice(c * LANES, (c + 1) * LANES)).T
        for q in range(LANES // freqs):
            k = c * (LANES // freqs) + q
            tail = jnp.zeros((filler, dim), F32)
            if k < len(values):
                one = jnp.broadcast_to(small[k : k + 1, :], (filler, dim))
                two = pltpu.roll(one, dim // 2, 1)
                tail = jnp.where(base == 0, jnp.where(left, one, two), 0.0)
                tail = jnp.where(base == 1, jnp.where(left, two, one), tail)
            tail_s[k] = jnp.concatenate([turned[q * freqs : (q + 1) * freqs, :], tail], axis=0)
    part = hidden
    m_ordered = ordered(m_s, slice(None))
    for r in range(0, 2 * hidden, part):
        acc_s[r : r + part, :] = dot_nt(bproj_s[r : r + part, :], m_ordered)
    acc_s[2 * hidden : 3 * hidden, :] = dot_nt(act_s[...], ordered(bo, slice(None)))
    left = lax.broadcasted_iota(jnp.int32, (out_rows, dim), 1) < dim // 2
    for y in range(far):
        for q in range(near // 2):
            chip = y * (near // 2) + q
            for dst, k in ((keep, 2 * chip + core), (send, 2 * chip + 1 - core)):
                weights = acc_s[pl.ds(pl.multiple_of(k * rows, 8), rows), :]
                block = jnp.concatenate([weights, tail_s[k]], axis=0)
                top, bottom = block[0:out_rows, :], block[out_rows : 2 * out_rows, :]
                dst[2 * q, y] = jnp.where(left, top, pltpu.roll(bottom, dim // 2, 1)).astype(BF16)
                dst[2 * q + 1, y] = jnp.where(left, pltpu.roll(top, dim // 2, 1), bottom).astype(BF16)


def out_kernel(level, act, wt, out):
    dim, span = level.shape[0], level.shape[1] // 2
    hidden = act.shape[0]
    ri = lax.broadcasted_iota(jnp.int32, (dim, dim), 0)
    ci = lax.broadcasted_iota(jnp.int32, (dim, dim), 1)
    turn = jnp.where(ri + ci == dim - 1, 1.0, 0.0).astype(BF16)
    z = level[...] + dot(wt[:, 2 * hidden : 3 * hidden], act[...])
    z = z.astype(BF16)
    out[0:dim, :] = z[:, 0:span]
    out[dim : 2 * dim, :] = dot(turn, z[:, span : 2 * span]).astype(BF16)


def gather_kernel(where_ref, lf, tok, msg):
    own_ch, group = lf.shape
    half = group // LANES // 2
    core = where_ref[1]
    tiles = []
    for c in range(half):
        at = pl.multiple_of((core * half + c) * LANES, LANES)
        tiles.append(lf[:, pl.ds(at, LANES)])
    ids = jnp.broadcast_to(tok[...].astype(F32), (8, tok.shape[1]))
    row = lax.broadcasted_iota(jnp.int32, (16, LANES), 0)
    last = jnp.zeros((16, LANES), F32)
    for j in range(tok.shape[1] // LANES):
        part = jnp.broadcast_to(ids[0:1, j * LANES : (j + 1) * LANES], (16, LANES))
        last = jnp.where(row == j, part, last)
    whole = jnp.concatenate(tiles + [last], axis=0).astype(BF16)
    for sh in range(msg.shape[0]):
        msg[sh] = whole


def prep_kernel(emb, taps, gin, gmid, cols, acat):
    dim = emb.shape[1]
    e = emb[...]
    scale = lax.rsqrt(jnp.sum(e * e, axis=1, keepdims=True) * (1.0 / dim) + 1e-06)
    ntab = (e * scale * gin[...]).astype(BF16).astype(F32)
    rows = [e[t : t + 1, :] for t in range(4)] + [taps[k : k + 1, :] for k in range(4)]
    rows += [ntab[t : t + 1, :] for t in range(4)] + [gin[...], gmid[...]]
    row = lax.broadcasted_iota(jnp.int32, (LANES, dim), 0)
    table = jnp.zeros((LANES, dim), F32)
    for i, r in enumerate(rows):
        table = jnp.where(row == i, r, table)
    cols[...] = table.T
    coefs = jnp.zeros((LANES, dim), F32)
    for k in range(4):
        for t in range(4):
            value = taps[k : k + 1, :] * ntab[t : t + 1, :]
            high = value.astype(BF16).astype(F32)
            at = 4 * k + t
            coefs = jnp.where((row == at) | (row == 32 + at), high, coefs)
            coefs = jnp.where(row == 16 + at, value - high, coefs)
    acat[...] = coefs.T[:, 0:48].astype(BF16)


def over_near_kernel(got, msg, *, rows, freqs):
    near, far, half, dim = got.shape
    own = msg.shape[1] - 8
    peers = msg.shape[0] // far
    lane = lax.broadcasted_iota(jnp.int32, (1, dim), 1)
    row = lax.broadcasted_iota(jnp.int32, (8, LANES), 0)
    for y in range(far):
        total = got[0, y].astype(F32)
        for i in range(1, near):
            total += got[i, y].astype(F32)
        bottom = pltpu.roll(total, dim // 2, 1)
        at = rows + freqs - half
        high = pltpu.roll(bottom, dim // 2, 1)[at + 1 : at + 2, :]
        small = jnp.where(lane < dim // 2, bottom[at : at + 1, :], high)
        both = jnp.concatenate([total, bottom], axis=0)
        both = jnp.concatenate([both, jnp.zeros((LANES - 2 * half, dim), F32)], axis=0)
        turned = both[:, 0 : 2 * LANES].T
        lines = jnp.zeros((8, LANES), F32)
        for j in range(dim // LANES):
            lines = jnp.where(row == j, small[:, j * LANES : (j + 1) * LANES], lines)
        for p in range(peers):
            part = turned[p * own : (p + 1) * own, :]
            msg[y * peers + p] = jnp.concatenate([part, lines], axis=0).astype(BF16)


def over_far_kernel(got, g_mlp, msg, *, freqs):
    total = got[0].astype(F32)
    for i in range(1, got.shape[0]):
        total += got[i].astype(F32)
    own, rows = g_mlp.shape
    g_mlp[...] = total[0:own, 0:rows]
    lane = lax.broadcasted_iota(jnp.int32, (own, LANES), 1)
    part = jnp.where(lane < freqs, pltpu.roll(total[0:own, :], LANES - rows, 1), 0.0)
    first = part[0:8, :]
    for j in range(1, own // 8):
        first += pltpu.roll(part[8 * j : 8 * j + 8, :], freqs * j, 1)
    whole = jnp.concatenate([first, total[own : own + 8, :]], axis=0).astype(BF16)
    for i in range(msg.shape[0]):
        msg[i] = whole


def final_kernel(got, g_filter, g_emb, g_gin, g_conv, g_mid):
    own, group = g_filter.shape
    dim = g_emb.shape[1]
    peers = got.shape[0]
    freqs = group // peers
    per = LANES // freqs
    lane = lax.broadcasted_iota(jnp.int32, (8, LANES), 1)
    lines = []
    for c in range(group // LANES):
        tiles = [jnp.zeros((8, LANES), F32) for _ in range(own // 8)]
        for q in range(per):
            x = got[c * per + q].astype(F32)
            if len(lines) < 10:
                lines.append([x[8 + j : 9 + j, :] for j in range(dim // LANES)])
            mine = (lane >= q * freqs) & (lane < (q + 1) * freqs)
            for j in range(own // 8):
                shift = (q - j) * freqs % LANES
                y = x[0:8, :] if shift == 0 else pltpu.roll(x[0:8, :], shift, 1)
                tiles[j] = jnp.where(mine, y, tiles[j])
        for j in range(own // 8):
            g_filter[8 * j : 8 * j + 8, c * LANES : (c + 1) * LANES] = tiles[j]
    for j in range(dim // LANES):
        lanes = slice(j * LANES, (j + 1) * LANES)
        for t in range(4):
            g_emb[t : t + 1, lanes] = lines[t][j]
            g_conv[t : t + 1, lanes] = lines[5 + t][j]
        g_gin[0:1, lanes] = lines[4][j]
        g_mid[0:1, lanes] = lines[9][j]


def split_to(x, axis):
    return lax.all_to_all(x, axis, 0, 0, tiled=True)


def swapped(x, axis, distance):
    return lax.ppermute(x, axis, [(i, i ^ distance) for i in range(lax.axis_size(axis))])


def added(a, b):
    return (a.astype(F32) + b.astype(F32)).astype(BF16)


def kernel_call(body, outs, ins, scratch=(), smem=0, flops=0, name=None):
    vmem = pl.BlockSpec(memory_space=pltpu.VMEM)
    moved = sum(x.size * x.dtype.itemsize for x in ins)
    moved += sum(int(np.prod(o.shape)) * o.dtype.itemsize for o in outs)
    return pl.pallas_call(
        body,
        out_shape=tuple(outs),
        in_specs=[pl.BlockSpec(memory_space=pltpu.SMEM)] * smem + [vmem] * (len(ins) - smem),
        out_specs=tuple([vmem] * len(outs)),
        scratch_shapes=list(scratch),
        compiler_params=pltpu.CompilerParams(vmem_limit_bytes=48 * 1024 * 1024),
        cost_estimate=pl.CostEstimate(flops=flops, bytes_accessed=moved, transcendentals=0),
        name=name,
    )(*ins)


def on_device(tokens, embedding, gain_in, conv_taps, long_filter, gain_mid, mlp_weights, cotangent):
    span = tokens.shape[1]
    dim = embedding.shape[1]
    hidden = mlp_weights.shape[0] // 3
    own_ch, group = long_filter.shape
    shards = lax.axis_size(SEQ)
    dps = lax.axis_size(DP)
    near, far = lax.axis_size(NEAR), lax.axis_size("dp_y")
    per_block = group // span
    groups = shards // per_block
    chunks = group // LANES
    half = chunks // 2
    place = lax.axis_index(SEQ)
    core = lax.axis_index("dp_c")
    shape = jax.ShapeDtypeStruct

    vec = jnp.stack([place, core, place // per_block])
    where = vec.astype(jnp.int32)
    (msg,) = kernel_call(
        gather_kernel,
        [shape((shards, half * own_ch + 16, LANES), BF16)],
        [where, long_filter, tokens],
        smem=1,
        name="gather",
    )
    gath = split_to(msg, SEQ)

    table = dct_table(group)
    qt = jnp.asarray(np.ascontiguousarray(table.T))
    inner = (place % per_block) * span
    qown = lax.dynamic_slice_in_dim(jnp.asarray(table), inner, span, 1)
    qtown = lax.dynamic_slice_in_dim(qt, inner, span, 0)
    wt = mlp_weights.T
    cols, acat = kernel_call(
        prep_kernel,
        [shape((dim, LANES), F32), shape((dim, 48), BF16)],
        [embedding, conv_taps.T, gain_in[None], gain_mid[None]],
        name="prep",
    )

    bo, ba = kernel_call(
        back_kernel,
        [shape((dim, 2 * span), BF16), shape((hidden, 2 * span), BF16)],
        [cotangent[0], mlp_weights],
        flops=4 * hidden * dim * span,
        name="back",
    )
    gath, bo, ba, wt, qown, qtown, acat, cols = lax.optimization_barrier(
        (gath, bo, ba, wt, qown, qtown, acat, cols)
    )
    gath_other = swapped(gath, "dp_c", 1)
    (ohq,) = kernel_call(
        partial(dct_kernel, half_rows=half * own_ch, per_block=per_block),
        [shape((2, groups, 48, group), BF16)],
        [gath, qt],
        flops=2 * 128 * group * group,
        name="bases",
    )
    own_rows = 3 * hidden // dps
    freqs = group // dps
    all_rows = own_rows + freqs + 8
    all_rows += -all_rows % 16
    half_rows = all_rows // 2
    act, level, keep, send = kernel_call(
        mid_kernel,
        [
            shape((hidden, 2 * span), BF16),
            shape((dim, 2 * span), F32),
            shape((near, far, half_rows, dim), BF16),
            shape((near, far, half_rows, dim), BF16),
        ],
        [where, gath, gath_other, tokens, cols, acat, mlp_weights, wt, qown, qtown, ohq, bo, ba],
        scratch=[
            pltpu.VMEM((chunks, dim, LANES), F32),
            pltpu.VMEM((dim, group), BF16),
            pltpu.VMEM((dim, group), BF16),
            pltpu.VMEM((dim, span), BF16),
            pltpu.VMEM((dim, 2 * span), BF16),
            pltpu.VMEM((2 * hidden, 2 * span), BF16),
            pltpu.VMEM((3 * hidden, dim), F32),
            pltpu.VMEM((dim, group), F32),
            pltpu.VMEM((dps, all_rows - own_rows, dim), F32),
        ],
        smem=1,
        flops=28 * hidden * dim * span,
        name="mid",
    )
    (layer,) = kernel_call(
        out_kernel, [shape((2 * dim, span), BF16)], [level, act, wt], flops=4 * hidden * dim * span, name="out"
    )
    block = split_to(added(keep, swapped(send, "dp_c", 1)), NEAR)
    (msg,) = kernel_call(
        partial(over_near_kernel, rows=own_rows, freqs=freqs),
        [shape((far * shards // 2, own_ch + 8, LANES), BF16)],
        [block],
        name="over_near",
    )
    grad_mlp, msg = kernel_call(
        partial(over_far_kernel, freqs=freqs),
        [shape((own_ch, own_rows), F32), shape((dps, 16, LANES), BF16)],
        [split_to(msg, FAR)],
        name="over_far",
    )
    grad_filter, grad_embedding, grad_gain_in, grad_conv, grad_gain_mid = kernel_call(
        final_kernel,
        [
            shape((own_ch, group), F32),
            shape((4, dim), F32),
            shape((1, dim), F32),
            shape((4, dim), F32),
            shape((1, dim), F32),
        ],
        [split_to(msg, DP)],
        name="final",
    )
    return (
        layer[None],
        grad_embedding,
        grad_gain_in[0],
        grad_conv.T,
        grad_filter,
        grad_gain_mid[0],
        grad_mlp.T,
    )


def solution(mesh):
    dps, seqs = mesh.devices.shape
    torus = Mesh(mesh.devices.reshape(dps // 8, 2, 2, 2, seqs // 4, 2, 2), DP + SEQ)
    return jax.shard_map(
        on_device,
        mesh=torus,
        in_specs=(P(DP, SEQ), P(), P(), P(), P(SEQ, None), P(), P(), P(DP, None, SEQ)),
        out_specs=(P(DP, None, SEQ), P(), P(), P(), P(SEQ, None), P(), P(DP, SEQ)),
        check_vma=False,
    )
```

```python
from functools import partial

import jax
import jax.numpy as jnp
import numpy as np
from jax import lax
from jax.experimental import pallas as pl
from jax.experimental.pallas import tpu as pltpu
from jax.sharding import Mesh
from jax.sharding import PartitionSpec as P

DP = ("dp_y", "dp_n", "dp_x", "dp_c")
SEQ = ("seq_z", "seq_n", "seq_x")
NEAR = ("dp_n", "dp_x", "seq_n")
FAR = ("dp_y", "seq_z", "seq_x")
F32, BF16 = jnp.float32, jnp.bfloat16
LANES = 128


def dct_table(length):
    freq = np.arange(length, dtype=np.int64)[:, None]
    place = np.arange(length, dtype=np.int64)[None, :]
    phase = (2 * place + 1) * freq % (4 * length)
    weight = np.where(freq == 0, np.sqrt(1.0 / length), np.sqrt(2.0 / length))
    return (weight * np.cos(np.pi * phase / (2 * length))).astype(np.float32).astype(jnp.bfloat16)


def dot(a, b):
    return jnp.dot(a, b, preferred_element_type=F32)


def dot_nt(a, b):
    return lax.dot_general(a, b, (((1,), (1,)), ((), ())), preferred_element_type=F32)


def onehot_rows(gath, groups, group, half_rows, per_block):
    shards = gath.shape[0]
    rows_of = 2
    ids = [gath[sh, half_rows : half_rows + 16, :].astype(F32) for sh in range(shards)]
    rows = [ids[sh][j : j + 1, :] for sh in range(shards) for j in range(rows_of)]
    outside = jnp.full((1, LANES), -1.0, F32)
    rows = [outside] + rows + [outside]
    per = per_block * rows_of
    width = group + 2 * LANES
    row = lax.broadcasted_iota(jnp.int32, (32, group), 0)
    want = jnp.where(row < 16, row % 4, 3 - row % 4).astype(F32)
    onehots = []
    for b in range(groups):
        pieces = rows[b * per : b * per + per + 2]
        ext = jnp.concatenate([jnp.broadcast_to(p, (8, LANES)) for p in pieces], axis=1)
        picked = jnp.zeros((32, group), F32)
        for j in range(8):
            shift = j if j < 4 else (width - (j - 4)) % width
            moved = ext if shift == 0 else pltpu.roll(ext, shift, 1)
            moved = jnp.broadcast_to(moved[0:1, LANES : LANES + group], (32, group))
            picked = jnp.where(row // 4 == j, moved, picked)
        onehots.append(jnp.where(picked == want, 1.0, 0.0).astype(BF16))
    return onehots


def dct_kernel(gath, qt, ohq, *, half_rows, per_block):
    _, groups, _, group = ohq.shape
    onehots = onehot_rows(gath, groups, group, half_rows, per_block)
    both = dot(jnp.concatenate(onehots, axis=0), qt[...])
    for b in range(groups):
        x = both[32 * b : 32 * b + 32, :]
        high = x.astype(BF16)
        low = (x - high.astype(F32)).astype(BF16)
        for s in range(2):
            o_high = high[16 * s : 16 * s + 16]
            o_low = low[16 * s : 16 * s + 16]
            ocat = jnp.concatenate([o_high, o_high, o_low], axis=0)
            ohq[s, b] = ocat


def back_kernel(cot, w, bo, ba):
    dim, span = cot.shape[0] // 2, cot.shape[1]
    ri = lax.broadcasted_iota(jnp.int32, (dim, dim), 0)
    ci = lax.broadcasted_iota(jnp.int32, (dim, dim), 1)
    turn = jnp.where(ri + ci == dim - 1, 1.0, 0.0).astype(BF16)
    bo[:, 0:span] = cot[0:dim, :]
    bo[:, span : 2 * span] = dot(turn, cot[dim : 2 * dim, :]).astype(BF16)
    hidden = ba.shape[0]
    for r in range(0, hidden, 256):
        ba[r : r + 256, :] = dot(w[2 * hidden + r : 2 * hidden + r + 256, :], bo[...]).astype(BF16)


def mid_kernel(
    where_ref, ga, gb, tok_ref, cols, acat, w, wt, qown, qtown, ohq, bo, ba,
    act_s, level_s, keep, send,
    lf_s, scaled_s, spec_s, df_s, m_s, bproj_s, acc_s, gf_s, tail_s,
):
    shards = ga.shape[0]
    chunks, dim, _ = lf_s.shape
    own_ch = dim // shards
    hidden = act_s.shape[0]
    span = tok_ref.shape[1]
    half = chunks // 2
    body_rows = half * own_ch
    core = where_ref[1]
    block = where_ref[2]
    near, far, out_rows, _ = keep.shape
    chips = near // 2 * far
    rows = (3 * hidden) // (2 * chips)
    freqs = chunks * LANES // (2 * chips)
    pair = 2 * own_ch
    order = list(range(0, shards // 2, 2)) + list(range(1, shards // 2, 2))

    def ordered(ref, lanes):
        return jnp.concatenate([ref[g * pair : (g + 1) * pair, lanes] for g in order], axis=0)

    for sh in range(shards):
        for c in range(half):
            src = slice(c * own_ch, (c + 1) * own_ch)
            dst = slice(sh * own_ch, (sh + 1) * own_ch)
            lf_s[core * half + c, dst, :] = ga[sh, 0:body_rows, :].astype(F32)[src, :]
            lf_s[(1 - core) * half + c, dst, :] = gb[sh, 0:body_rows, :].astype(F32)[src, :]
    emb = cols[:, 0:4]
    gmid = cols[:, 13:14]
    tok = tok_ref[...].astype(F32)
    step = 128
    gmid_part = jnp.zeros((dim, 1), F32)
    direct = jnp.zeros((dim, 16), F32)
    taps_part = [jnp.zeros((step, 16), F32) for _ in range(dim // step)]
    for s in range(2):
        here = slice(s * span, (s + 1) * span)
        ocat = ohq[s, block]
        for r in range(0, dim, step):
            spec = dot(acat[r : r + step, :], ocat).astype(BF16)
            spec_s[r : r + step, :] = spec
            spec = spec.astype(F32)
            for c in range(chunks):
                lanes = slice(c * LANES, (c + 1) * LANES)
                scaled_s[r : r + step, lanes] = (lf_s[c, r : r + step, :] * spec[:, lanes]).astype(BF16)
        filt = dot(scaled_s[...], qown[...]).astype(BF16).astype(F32)
        ids = tok if s == 0 else 3.0 - tok
        resid = jnp.broadcast_to(emb[:, 3:4], (dim, span))
        for t in range(3):
            resid = jnp.where(ids == float(t), emb[:, t : t + 1], resid)
        level = resid + filt
        level_s[:, here] = level
        scale = lax.rsqrt(jnp.sum(level * level, axis=0, keepdims=True) * (1.0 / dim) + 1e-06)
        m_s[:, here] = (level * scale * gmid).astype(BF16)
        normed = m_s[:, here]
        part = 256
        for h in range(0, hidden, part):
            gate = dot(w[h : h + part, :], normed).astype(BF16).astype(F32)
            up = dot(w[hidden + h : hidden + h + part, :], normed).astype(BF16).astype(F32)
            b = ba[h : h + part, here].astype(F32)
            sig = jax.nn.sigmoid(gate)
            swish = gate * sig
            act_s[h : h + part, here] = (swish * up).astype(BF16)
            bproj_s[h : h + part, here] = (b * up * sig * (1.0 + gate * (1.0 - sig))).astype(BF16)
            bproj_s[hidden + h : hidden + h + part, here] = (b * swish).astype(BF16)
        bmid = dot(wt[:, 0 : 2 * hidden], bproj_s[:, here]).astype(BF16).astype(F32)
        level = level_s[:, here]
        gmid_part += jnp.sum(bmid * level * scale, axis=1, keepdims=True)
        weighed = bmid * gmid
        pull = jnp.sum(weighed * level, axis=0, keepdims=True)
        dlevel = (
            bo[:, here].astype(F32)
            + scale * weighed
            - level * (scale * scale * scale * pull * (1.0 / dim))
        )
        dfilt = dlevel.astype(BF16)
        df_s[...] = dfilt
        base = lax.broadcasted_iota(jnp.int32, (16, span), 0).astype(F32)
        mine = jnp.where(ids == base, 1.0, 0.0).astype(BF16)
        direct += dot_nt(dfilt, mine)
        for i, r in enumerate(range(0, dim, step)):
            ds = dot(df_s[r : r + step, :], qtown[...])
            term = ds * spec_s[r : r + step, :].astype(F32)
            if s == 0:
                gf_s[r : r + step, :] = term
            else:
                gf_s[r : r + step, :] += term
            for c in range(chunks):
                lanes = slice(c * LANES, (c + 1) * LANES)
                scaled_s[r : r + step, lanes] = (lf_s[c, r : r + step, :] * ds[:, lanes]).astype(BF16)
            both = dot_nt(scaled_s[r : r + step, :], ocat[16:48, :])
            taps_part[i] += both[:, 0:16] + both[:, 16:32]
    taps = cols[:, 4:8]
    ntab = cols[:, 8:12]
    gin = cols[:, 12:13]
    g = jnp.concatenate(taps_part, axis=0)
    dn = jnp.zeros((dim, 4), F32)
    conv = []
    for k in range(4):
        gk = g[:, 4 * k : 4 * k + 4]
        dn += taps[:, k : k + 1] * gk
        conv.append(jnp.sum(ntab * gk, axis=1, keepdims=True))
    escale = lax.rsqrt(jnp.sum(emb * emb, axis=0, keepdims=True) * (1.0 / dim) + 1e-06)
    epull = jnp.sum(gin * dn * emb, axis=0, keepdims=True)
    demb = escale * gin * dn - emb * (escale * escale * escale * epull * (1.0 / dim))
    demb += direct[:, 0:4]
    dgin = jnp.sum(dn * emb * escale, axis=1, keepdims=True)
    lane = lax.broadcasted_iota(jnp.int32, (dim, LANES), 1)
    small = jnp.zeros((dim, LANES), F32)
    values = [demb[:, t : t + 1] for t in range(4)] + [dgin] + conv + [gmid_part]
    for i, val in enumerate(values):
        small = jnp.where(lane == i, val, small)
    small = small.T
    filler = 2 * out_rows - rows - freqs
    base = lax.broadcasted_iota(jnp.int32, (filler, dim), 0)
    left = lax.broadcasted_iota(jnp.int32, (filler, dim), 1) < dim // 2
    for c in range(chunks):
        turned = ordered(gf_s, slice(c * LANES, (c + 1) * LANES)).T
        for q in range(LANES // freqs):
            k = c * (LANES // freqs) + q
            tail = jnp.zeros((filler, dim), F32)
            if k < len(values):
                one = jnp.broadcast_to(small[k : k + 1, :], (filler, dim))
                two = pltpu.roll(one, dim // 2, 1)
                tail = jnp.where(base == 0, jnp.where(left, one, two), 0.0)
                tail = jnp.where(base == 1, jnp.where(left, two, one), tail)
            tail_s[k] = jnp.concatenate([turned[q * freqs : (q + 1) * freqs, :], tail], axis=0)
    part = hidden
    m_ordered = ordered(m_s, slice(None))
    for r in range(0, 2 * hidden, part):
        acc_s[r : r + part, :] = dot_nt(bproj_s[r : r + part, :], m_ordered)
    acc_s[2 * hidden : 3 * hidden, :] = dot_nt(act_s[...], ordered(bo, slice(None)))
    left = lax.broadcasted_iota(jnp.int32, (out_rows, dim), 1) < dim // 2
    for y in range(far):
        for q in range(near // 2):
            chip = y * (near // 2) + q
            for dst, k in ((keep, 2 * chip + core), (send, 2 * chip + 1 - core)):
                weights = acc_s[pl.ds(pl.multiple_of(k * rows, 8), rows), :]
                block = jnp.concatenate([weights, tail_s[k]], axis=0)
                top, bottom = block[0:out_rows, :], block[out_rows : 2 * out_rows, :]
                dst[2 * q, y] = jnp.where(left, top, pltpu.roll(bottom, dim // 2, 1)).astype(BF16)
                dst[2 * q + 1, y] = jnp.where(left, pltpu.roll(top, dim // 2, 1), bottom).astype(BF16)


def out_kernel(level, act, wt, out):
    dim, span = level.shape[0], level.shape[1] // 2
    hidden = act.shape[0]
    ri = lax.broadcasted_iota(jnp.int32, (dim, dim), 0)
    ci = lax.broadcasted_iota(jnp.int32, (dim, dim), 1)
    turn = jnp.where(ri + ci == dim - 1, 1.0, 0.0).astype(BF16)
    z = level[...] + dot(wt[:, 2 * hidden : 3 * hidden], act[...])
    z = z.astype(BF16)
    out[0:dim, :] = z[:, 0:span]
    out[dim : 2 * dim, :] = dot(turn, z[:, span : 2 * span]).astype(BF16)


def gather_kernel(where_ref, lf, tok, msg):
    own_ch, group = lf.shape
    half = group // LANES // 2
    core = where_ref[1]
    tiles = []
    for c in range(half):
        at = pl.multiple_of((core * half + c) * LANES, LANES)
        tiles.append(lf[:, pl.ds(at, LANES)])
    ids = jnp.broadcast_to(tok[...].astype(F32), (8, tok.shape[1]))
    row = lax.broadcasted_iota(jnp.int32, (16, LANES), 0)
    last = jnp.zeros((16, LANES), F32)
    for j in range(tok.shape[1] // LANES):
        part = jnp.broadcast_to(ids[0:1, j * LANES : (j + 1) * LANES], (16, LANES))
        last = jnp.where(row == j, part, last)
    whole = jnp.concatenate(tiles + [last], axis=0).astype(BF16)
    for sh in range(msg.shape[0]):
        msg[sh] = whole


def prep_kernel(emb, taps, gin, gmid, cols, acat):
    dim = emb.shape[1]
    e = emb[...]
    scale = lax.rsqrt(jnp.sum(e * e, axis=1, keepdims=True) * (1.0 / dim) + 1e-06)
    ntab = (e * scale * gin[...]).astype(BF16).astype(F32)
    rows = [e[t : t + 1, :] for t in range(4)] + [taps[k : k + 1, :] for k in range(4)]
    rows += [ntab[t : t + 1, :] for t in range(4)] + [gin[...], gmid[...]]
    row = lax.broadcasted_iota(jnp.int32, (LANES, dim), 0)
    table = jnp.zeros((LANES, dim), F32)
    for i, r in enumerate(rows):
        table = jnp.where(row == i, r, table)
    cols[...] = table.T
    coefs = jnp.zeros((LANES, dim), F32)
    for k in range(4):
        for t in range(4):
            value = taps[k : k + 1, :] * ntab[t : t + 1, :]
            high = value.astype(BF16).astype(F32)
            at = 4 * k + t
            coefs = jnp.where((row == at) | (row == 32 + at), high, coefs)
            coefs = jnp.where(row == 16 + at, value - high, coefs)
    acat[...] = coefs.T[:, 0:48].astype(BF16)


def over_near_kernel(got, msg, *, rows, freqs):
    near, far, half, dim = got.shape
    own = msg.shape[1]
    peers = msg.shape[0] // far
    free = rows + freqs
    lane = lax.broadcasted_iota(jnp.int32, (1, dim), 1)
    row = lax.broadcasted_iota(jnp.int32, (own, LANES), 0)
    spare = lax.broadcasted_iota(jnp.int32, (own, LANES), 1) >= free
    for y in range(far):
        total = got[0, y].astype(F32)
        for i in range(1, near):
            total += got[i, y].astype(F32)
        bottom = pltpu.roll(total, dim // 2, 1)
        at = rows + freqs - half
        high = pltpu.roll(bottom, dim // 2, 1)[at + 1 : at + 2, :]
        small = jnp.where(lane < dim // 2, bottom[at : at + 1, :], high)
        both = jnp.concatenate([total, bottom], axis=0)
        both = jnp.concatenate([both, jnp.zeros((LANES - 2 * half, dim), F32)], axis=0)
        turned = both[:, 0 : 2 * LANES].T
        wide = jnp.broadcast_to(small, (8, dim))
        lines = jnp.zeros((own, LANES), F32)
        for m in range(dim // own):
            moved = pltpu.roll(wide, (free - own * m) % dim, 1)[0:1, 0:LANES]
            lines = jnp.where(row == m, moved, lines)
        for p in range(peers):
            part = turned[p * own : (p + 1) * own, :]
            msg[y * peers + p] = jnp.where(spare, lines, part).astype(BF16)


def over_far_kernel(got, g_mlp, msg, *, freqs):
    total = got[0].astype(F32)
    for i in range(1, got.shape[0]):
        total += got[i].astype(F32)
    own, rows = g_mlp.shape
    g_mlp[...] = total[0:own, 0:rows]
    lane = lax.broadcasted_iota(jnp.int32, (own, LANES), 1)
    part = jnp.where(lane < freqs, pltpu.roll(total[0:own, :], LANES - rows, 1), 0.0)
    first = part[0:8, :]
    for j in range(1, own // 8):
        first += pltpu.roll(part[8 * j : 8 * j + 8, :], freqs * j, 1)
    free = rows + freqs
    dim = 3 * LANES
    lane = lax.broadcasted_iota(jnp.int32, (8, LANES), 1)
    small = jnp.zeros((8, dim), F32)
    for m in range(dim // own):
        line = jnp.broadcast_to(total[m : m + 1, :], (8, LANES))
        line = jnp.where((lane >= free) & (lane < free + own), line, 0.0)
        wide = jnp.concatenate([line, jnp.zeros((8, dim - LANES), F32)], axis=1)
        shift = (own * m - free) % dim
        small += wide if shift == 0 else pltpu.roll(wide, shift, 1)
    row = lax.broadcasted_iota(jnp.int32, (8, LANES), 0)
    lines = jnp.zeros((8, LANES), F32)
    for j in range(dim // LANES):
        lines = jnp.where(row == j, small[:, j * LANES : (j + 1) * LANES], lines)
    whole = jnp.concatenate([first, lines], axis=0).astype(BF16)
    for i in range(msg.shape[0]):
        msg[i] = whole


def final_kernel(got, g_filter, g_emb, g_gin, g_conv, g_mid):
    own, group = g_filter.shape
    dim = g_emb.shape[1]
    peers = got.shape[0]
    freqs = group // peers
    per = LANES // freqs
    lane = lax.broadcasted_iota(jnp.int32, (8, LANES), 1)
    lines = []
    for c in range(group // LANES):
        tiles = [jnp.zeros((8, LANES), F32) for _ in range(own // 8)]
        for q in range(per):
            x = got[c * per + q].astype(F32)
            if len(lines) < 10:
                lines.append([x[8 + j : 9 + j, :] for j in range(dim // LANES)])
            mine = (lane >= q * freqs) & (lane < (q + 1) * freqs)
            for j in range(own // 8):
                shift = (q - j) * freqs % LANES
                y = x[0:8, :] if shift == 0 else pltpu.roll(x[0:8, :], shift, 1)
                tiles[j] = jnp.where(mine, y, tiles[j])
        for j in range(own // 8):
            g_filter[8 * j : 8 * j + 8, c * LANES : (c + 1) * LANES] = tiles[j]
    for j in range(dim // LANES):
        lanes = slice(j * LANES, (j + 1) * LANES)
        for t in range(4):
            g_emb[t : t + 1, lanes] = lines[t][j]
            g_conv[t : t + 1, lanes] = lines[5 + t][j]
    g_gin[...] = jnp.concatenate(lines[4], axis=1)[0, :]
    g_mid[...] = jnp.concatenate(lines[9], axis=1)[0, :]


def split_to(x, axis):
    return lax.all_to_all(x, axis, 0, 0, tiled=True)


def swapped(x, axis, distance):
    return lax.ppermute(x, axis, [(i, i ^ distance) for i in range(lax.axis_size(axis))])


def added(a, b):
    return (a.astype(F32) + b.astype(F32)).astype(BF16)


def kernel_call(body, outs, ins, scratch=(), smem=0, flops=0, name=None):
    vmem = pl.BlockSpec(memory_space=pltpu.VMEM)
    moved = sum(x.size * x.dtype.itemsize for x in ins)
    moved += sum(int(np.prod(o.shape)) * o.dtype.itemsize for o in outs)
    return pl.pallas_call(
        body,
        out_shape=tuple(outs),
        in_specs=[pl.BlockSpec(memory_space=pltpu.SMEM)] * smem + [vmem] * (len(ins) - smem),
        out_specs=tuple([vmem] * len(outs)),
        scratch_shapes=list(scratch),
        compiler_params=pltpu.CompilerParams(vmem_limit_bytes=48 * 1024 * 1024),
        cost_estimate=pl.CostEstimate(flops=flops, bytes_accessed=moved, transcendentals=0),
        name=name,
    )(*ins)


def on_device(tokens, embedding, gain_in, conv_taps, long_filter, gain_mid, mlp_weights, cotangent):
    span = tokens.shape[1]
    dim = embedding.shape[1]
    hidden = mlp_weights.shape[0] // 3
    own_ch, group = long_filter.shape
    shards = lax.axis_size(SEQ)
    dps = lax.axis_size(DP)
    near, far = lax.axis_size(NEAR), lax.axis_size("dp_y")
    per_block = group // span
    groups = shards // per_block
    chunks = group // LANES
    half = chunks // 2
    place = lax.axis_index(SEQ)
    core = lax.axis_index("dp_c")
    shape = jax.ShapeDtypeStruct

    vec = jnp.stack([place, core, place // per_block])
    where = vec.astype(jnp.int32)
    (msg,) = kernel_call(
        gather_kernel,
        [shape((shards, half * own_ch + 16, LANES), BF16)],
        [where, long_filter, tokens],
        smem=1,
        name="gather",
    )
    gath = split_to(msg, SEQ)

    table = dct_table(group)
    qt = jnp.asarray(np.ascontiguousarray(table.T))
    inner = (place % per_block) * span
    qown = lax.dynamic_slice_in_dim(jnp.asarray(table), inner, span, 1)
    qtown = lax.dynamic_slice_in_dim(qt, inner, span, 0)
    wt = mlp_weights.T
    cols, acat = kernel_call(
        prep_kernel,
        [shape((dim, LANES), F32), shape((dim, 48), BF16)],
        [embedding, conv_taps.T, gain_in[None], gain_mid[None]],
        name="prep",
    )

    bo, ba = kernel_call(
        back_kernel,
        [shape((dim, 2 * span), BF16), shape((hidden, 2 * span), BF16)],
        [cotangent[0], mlp_weights],
        flops=4 * hidden * dim * span,
        name="back",
    )
    gath, bo, ba, wt, qown, qtown, acat, cols = lax.optimization_barrier(
        (gath, bo, ba, wt, qown, qtown, acat, cols)
    )
    gath_other = swapped(gath, "dp_c", 1)
    (ohq,) = kernel_call(
        partial(dct_kernel, half_rows=half * own_ch, per_block=per_block),
        [shape((2, groups, 48, group), BF16)],
        [gath, qt],
        flops=2 * 128 * group * group,
        name="bases",
    )
    own_rows = 3 * hidden // dps
    freqs = group // dps
    all_rows = own_rows + freqs + 8
    all_rows += -all_rows % 16
    half_rows = all_rows // 2
    act, level, keep, send = kernel_call(
        mid_kernel,
        [
            shape((hidden, 2 * span), BF16),
            shape((dim, 2 * span), F32),
            shape((near, far, half_rows, dim), BF16),
            shape((near, far, half_rows, dim), BF16),
        ],
        [where, gath, gath_other, tokens, cols, acat, mlp_weights, wt, qown, qtown, ohq, bo, ba],
        scratch=[
            pltpu.VMEM((chunks, dim, LANES), F32),
            pltpu.VMEM((dim, group), BF16),
            pltpu.VMEM((dim, group), BF16),
            pltpu.VMEM((dim, span), BF16),
            pltpu.VMEM((dim, 2 * span), BF16),
            pltpu.VMEM((2 * hidden, 2 * span), BF16),
            pltpu.VMEM((3 * hidden, dim), F32),
            pltpu.VMEM((dim, group), F32),
            pltpu.VMEM((dps, all_rows - own_rows, dim), F32),
        ],
        smem=1,
        flops=28 * hidden * dim * span,
        name="mid",
    )
    (layer,) = kernel_call(
        out_kernel, [shape((2 * dim, span), BF16)], [level, act, wt], flops=4 * hidden * dim * span, name="out"
    )
    block = split_to(added(keep, swapped(send, "dp_c", 1)), NEAR)
    (msg,) = kernel_call(
        partial(over_near_kernel, rows=own_rows, freqs=freqs),
        [shape((far * shards // 2, own_ch, LANES), BF16)],
        [block],
        name="over_near",
    )
    grad_mlp, msg = kernel_call(
        partial(over_far_kernel, freqs=freqs),
        [shape((own_ch, own_rows), F32), shape((dps, 16, LANES), BF16)],
        [split_to(msg, FAR)],
        name="over_far",
    )
    grad_filter, grad_embedding, grad_gain_in, grad_conv, grad_gain_mid = kernel_call(
        final_kernel,
        [
            shape((own_ch, group), F32),
            shape((4, dim), F32),
            shape((dim,), F32),
            shape((4, dim), F32),
            shape((dim,), F32),
        ],
        [split_to(msg, DP)],
        name="final",
    )
    return (
        layer[None],
        grad_embedding,
        grad_gain_in,
        grad_conv.T,
        grad_filter,
        grad_gain_mid,
        grad_mlp.T,
    )


def solution(mesh):
    dps, seqs = mesh.devices.shape
    torus = Mesh(mesh.devices.reshape(dps // 8, 2, 2, 2, seqs // 4, 2, 2), DP + SEQ)
    return jax.shard_map(
        on_device,
        mesh=torus,
        in_specs=(P(DP, SEQ), P(), P(), P(), P(SEQ, None), P(), P(), P(DP, None, SEQ)),
        out_specs=(P(DP, None, SEQ), P(), P(), P(), P(SEQ, None), P(), P(DP, SEQ)),
        check_vma=False,
    )
```

```python
from functools import partial

import jax
import jax.numpy as jnp
import numpy as np
from jax import lax
from jax.experimental import pallas as pl
from jax.experimental.pallas import tpu as pltpu
from jax.sharding import Mesh
from jax.sharding import PartitionSpec as P

DP = ("dp_y", "dp_n", "dp_x", "dp_c")
SEQ = ("seq_z", "seq_n", "seq_x")
NEAR = ("dp_n", "dp_x", "seq_n")
FAR = ("dp_y", "seq_z", "seq_x")
F32, BF16 = jnp.float32, jnp.bfloat16
LANES = 128


def dct_table(length):
    freq = np.arange(length, dtype=np.int64)[:, None]
    place = np.arange(length, dtype=np.int64)[None, :]
    phase = (2 * place + 1) * freq % (4 * length)
    weight = np.where(freq == 0, np.sqrt(1.0 / length), np.sqrt(2.0 / length))
    return (weight * np.cos(np.pi * phase / (2 * length))).astype(np.float32).astype(jnp.bfloat16)


def dot(a, b):
    return jnp.dot(a, b, preferred_element_type=F32)


def dot_nt(a, b):
    return lax.dot_general(a, b, (((1,), (1,)), ((), ())), preferred_element_type=F32)


def onehot_rows(gath, groups, group, half_rows, per_block):
    shards = gath.shape[0]
    rows_of = 2
    ids = [gath[sh, half_rows : half_rows + 16, :].astype(F32) for sh in range(shards)]
    rows = [ids[sh][j : j + 1, :] for sh in range(shards) for j in range(rows_of)]
    outside = jnp.full((1, LANES), -1.0, F32)
    rows = [outside] + rows + [outside]
    per = per_block * rows_of
    width = group + 2 * LANES
    row = lax.broadcasted_iota(jnp.int32, (32, group), 0)
    want = jnp.where(row < 16, row % 4, 3 - row % 4).astype(F32)
    onehots = []
    for b in range(groups):
        pieces = rows[b * per : b * per + per + 2]
        ext = jnp.concatenate([jnp.broadcast_to(p, (8, LANES)) for p in pieces], axis=1)
        picked = jnp.zeros((32, group), F32)
        for j in range(8):
            shift = j if j < 4 else (width - (j - 4)) % width
            moved = ext if shift == 0 else pltpu.roll(ext, shift, 1)
            moved = jnp.broadcast_to(moved[0:1, LANES : LANES + group], (32, group))
            picked = jnp.where(row // 4 == j, moved, picked)
        onehots.append(jnp.where(picked == want, 1.0, 0.0).astype(BF16))
    return onehots


def dct_kernel(gath, qt, ohq, *, half_rows, per_block):
    _, groups, _, group = ohq.shape
    onehots = onehot_rows(gath, groups, group, half_rows, per_block)
    both = dot(jnp.concatenate(onehots, axis=0), qt[...])
    for b in range(groups):
        x = both[32 * b : 32 * b + 32, :]
        high = x.astype(BF16)
        low = (x - high.astype(F32)).astype(BF16)
        for s in range(2):
            o_high = high[16 * s : 16 * s + 16]
            o_low = low[16 * s : 16 * s + 16]
            ocat = jnp.concatenate([o_high, o_high, o_low], axis=0)
            ohq[s, b] = ocat


def back_kernel(cot, w, bo, ba):
    dim, span = cot.shape[0] // 2, cot.shape[1]
    ri = lax.broadcasted_iota(jnp.int32, (dim, dim), 0)
    ci = lax.broadcasted_iota(jnp.int32, (dim, dim), 1)
    turn = jnp.where(ri + ci == dim - 1, 1.0, 0.0).astype(BF16)
    bo[:, 0:span] = cot[0:dim, :]
    bo[:, span : 2 * span] = dot(turn, cot[dim : 2 * dim, :]).astype(BF16)
    hidden = ba.shape[0]
    for r in range(0, hidden, 256):
        ba[r : r + 256, :] = dot(w[2 * hidden + r : 2 * hidden + r + 256, :], bo[...]).astype(BF16)


def mid_kernel(
    where_ref, ga, gb, tok_ref, cols, acat, w, wt, qown, qtown, ohq, bo, ba,
    act_s, level_s, keep, send,
    lf_s, scaled_s, spec_s, df_s, m_s, bproj_s, acc_s, gf_s, tail_s,
):
    shards = ga.shape[0]
    chunks, dim, _ = lf_s.shape
    own_ch = dim // shards
    hidden = act_s.shape[0]
    span = tok_ref.shape[1]
    half = chunks // 2
    body_rows = half * own_ch
    core = where_ref[1]
    block = where_ref[2]
    near, far, out_rows, _ = keep.shape
    chips = near // 2 * far
    rows = (3 * hidden) // (2 * chips)
    freqs = chunks * LANES // (2 * chips)
    pair = 2 * own_ch
    order = list(range(0, shards // 2, 2)) + list(range(1, shards // 2, 2))

    def ordered(ref, lanes):
        return jnp.concatenate([ref[g * pair : (g + 1) * pair, lanes] for g in order], axis=0)

    for sh in range(shards):
        for c in range(half):
            src = slice(c * own_ch, (c + 1) * own_ch)
            dst = slice(sh * own_ch, (sh + 1) * own_ch)
            lf_s[core * half + c, dst, :] = ga[sh, 0:body_rows, :].astype(F32)[src, :]
            lf_s[(1 - core) * half + c, dst, :] = gb[sh, 0:body_rows, :].astype(F32)[src, :]
    emb = cols[:, 0:4]
    gmid = cols[:, 13:14]
    tok = tok_ref[...].astype(F32)
    step = 384
    gmid_part = jnp.zeros((dim, 1), F32)
    direct = jnp.zeros((dim, 16), F32)
    taps_part = [jnp.zeros((step, 16), F32) for _ in range(dim // step)]
    for s in range(2):
        here = slice(s * span, (s + 1) * span)
        ocat = ohq[s, block]
        for r in range(0, dim, step):
            spec = dot(acat[r : r + step, :], ocat).astype(BF16)
            spec_s[r : r + step, :] = spec
            spec = spec.astype(F32)
            for c in range(chunks):
                lanes = slice(c * LANES, (c + 1) * LANES)
                scaled_s[r : r + step, lanes] = (lf_s[c, r : r + step, :] * spec[:, lanes]).astype(BF16)
        filt = dot(scaled_s[...], qown[...]).astype(BF16).astype(F32)
        ids = tok if s == 0 else 3.0 - tok
        resid = jnp.broadcast_to(emb[:, 3:4], (dim, span))
        for t in range(3):
            resid = jnp.where(ids == float(t), emb[:, t : t + 1], resid)
        level = resid + filt
        level_s[:, here] = level
        scale = lax.rsqrt(jnp.sum(level * level, axis=0, keepdims=True) * (1.0 / dim) + 1e-06)
        m_s[:, here] = (level * scale * gmid).astype(BF16)
        normed = m_s[:, here]
        part = 256
        for h in range(0, hidden, part):
            gate = dot(w[h : h + part, :], normed).astype(BF16).astype(F32)
            up = dot(w[hidden + h : hidden + h + part, :], normed).astype(BF16).astype(F32)
            b = ba[h : h + part, here].astype(F32)
            sig = jax.nn.sigmoid(gate)
            swish = gate * sig
            act_s[h : h + part, here] = (swish * up).astype(BF16)
            bproj_s[h : h + part, here] = (b * up * sig * (1.0 + gate * (1.0 - sig))).astype(BF16)
            bproj_s[hidden + h : hidden + h + part, here] = (b * swish).astype(BF16)
        bmid = dot(wt[:, 0 : 2 * hidden], bproj_s[:, here]).astype(BF16).astype(F32)
        level = level_s[:, here]
        gmid_part += jnp.sum(bmid * level * scale, axis=1, keepdims=True)
        weighed = bmid * gmid
        pull = jnp.sum(weighed * level, axis=0, keepdims=True)
        dlevel = (
            bo[:, here].astype(F32)
            + scale * weighed
            - level * (scale * scale * scale * pull * (1.0 / dim))
        )
        dfilt = dlevel.astype(BF16)
        df_s[...] = dfilt
        base = lax.broadcasted_iota(jnp.int32, (16, span), 0).astype(F32)
        mine = jnp.where(ids == base, 1.0, 0.0).astype(BF16)
        direct += dot_nt(dfilt, mine)
        for i, r in enumerate(range(0, dim, step)):
            ds = dot(df_s[r : r + step, :], qtown[...])
            term = ds * spec_s[r : r + step, :].astype(F32)
            if s == 0:
                gf_s[r : r + step, :] = term
            else:
                gf_s[r : r + step, :] += term
            for c in range(chunks):
                lanes = slice(c * LANES, (c + 1) * LANES)
                scaled_s[r : r + step, lanes] = (lf_s[c, r : r + step, :] * ds[:, lanes]).astype(BF16)
            both = dot_nt(scaled_s[r : r + step, :], ocat[16:48, :])
            taps_part[i] += both[:, 0:16] + both[:, 16:32]
    taps = cols[:, 4:8]
    ntab = cols[:, 8:12]
    gin = cols[:, 12:13]
    g = jnp.concatenate(taps_part, axis=0)
    dn = jnp.zeros((dim, 4), F32)
    conv = []
    for k in range(4):
        gk = g[:, 4 * k : 4 * k + 4]
        dn += taps[:, k : k + 1] * gk
        conv.append(jnp.sum(ntab * gk, axis=1, keepdims=True))
    escale = lax.rsqrt(jnp.sum(emb * emb, axis=0, keepdims=True) * (1.0 / dim) + 1e-06)
    epull = jnp.sum(gin * dn * emb, axis=0, keepdims=True)
    demb = escale * gin * dn - emb * (escale * escale * escale * epull * (1.0 / dim))
    demb += direct[:, 0:4]
    dgin = jnp.sum(dn * emb * escale, axis=1, keepdims=True)
    lane = lax.broadcasted_iota(jnp.int32, (dim, LANES), 1)
    small = jnp.zeros((dim, LANES), F32)
    values = [demb[:, t : t + 1] for t in range(4)] + [dgin] + conv + [gmid_part]
    for i, val in enumerate(values):
        small = jnp.where(lane == i, val, small)
    small = small.T
    filler = 2 * out_rows - rows - freqs
    base = lax.broadcasted_iota(jnp.int32, (filler, dim), 0)
    left = lax.broadcasted_iota(jnp.int32, (filler, dim), 1) < dim // 2
    for c in range(chunks):
        turned = ordered(gf_s, slice(c * LANES, (c + 1) * LANES)).T
        for q in range(LANES // freqs):
            k = c * (LANES // freqs) + q
            tail = jnp.zeros((filler, dim), F32)
            if k < len(values):
                one = jnp.broadcast_to(small[k : k + 1, :], (filler, dim))
                two = pltpu.roll(one, dim // 2, 1)
                tail = jnp.where(base == 0, jnp.where(left, one, two), 0.0)
                tail = jnp.where(base == 1, jnp.where(left, two, one), tail)
            tail_s[k] = jnp.concatenate([turned[q * freqs : (q + 1) * freqs, :], tail], axis=0)
    part = hidden
    m_ordered = ordered(m_s, slice(None))
    for r in range(0, 2 * hidden, part):
        acc_s[r : r + part, :] = dot_nt(bproj_s[r : r + part, :], m_ordered)
    acc_s[2 * hidden : 3 * hidden, :] = dot_nt(act_s[...], ordered(bo, slice(None)))
    left = lax.broadcasted_iota(jnp.int32, (out_rows, dim), 1) < dim // 2
    for y in range(far):
        for q in range(near // 2):
            chip = y * (near // 2) + q
            for dst, k in ((keep, 2 * chip + core), (send, 2 * chip + 1 - core)):
                weights = acc_s[pl.ds(pl.multiple_of(k * rows, 8), rows), :]
                block = jnp.concatenate([weights, tail_s[k]], axis=0)
                top, bottom = block[0:out_rows, :], block[out_rows : 2 * out_rows, :]
                dst[2 * q, y] = jnp.where(left, top, pltpu.roll(bottom, dim // 2, 1)).astype(BF16)
                dst[2 * q + 1, y] = jnp.where(left, pltpu.roll(top, dim // 2, 1), bottom).astype(BF16)


def out_kernel(level, act, wt, out):
    dim, span = level.shape[0], level.shape[1] // 2
    hidden = act.shape[0]
    ri = lax.broadcasted_iota(jnp.int32, (dim, dim), 0)
    ci = lax.broadcasted_iota(jnp.int32, (dim, dim), 1)
    turn = jnp.where(ri + ci == dim - 1, 1.0, 0.0).astype(BF16)
    z = level[...] + dot(wt[:, 2 * hidden : 3 * hidden], act[...])
    z = z.astype(BF16)
    out[0:dim, :] = z[:, 0:span]
    out[dim : 2 * dim, :] = dot(turn, z[:, span : 2 * span]).astype(BF16)


def gather_kernel(where_ref, lf, tok, msg):
    own_ch, group = lf.shape
    half = group // LANES // 2
    core = where_ref[1]
    tiles = []
    for c in range(half):
        at = pl.multiple_of((core * half + c) * LANES, LANES)
        tiles.append(lf[:, pl.ds(at, LANES)])
    ids = jnp.broadcast_to(tok[...].astype(F32), (8, tok.shape[1]))
    row = lax.broadcasted_iota(jnp.int32, (16, LANES), 0)
    last = jnp.zeros((16, LANES), F32)
    for j in range(tok.shape[1] // LANES):
        part = jnp.broadcast_to(ids[0:1, j * LANES : (j + 1) * LANES], (16, LANES))
        last = jnp.where(row == j, part, last)
    whole = jnp.concatenate(tiles + [last], axis=0).astype(BF16)
    for sh in range(msg.shape[0]):
        msg[sh] = whole


def prep_kernel(emb, taps, gin, gmid, cols, acat):
    dim = emb.shape[1]
    e = emb[...]
    scale = lax.rsqrt(jnp.sum(e * e, axis=1, keepdims=True) * (1.0 / dim) + 1e-06)
    ntab = (e * scale * gin[...]).astype(BF16).astype(F32)
    rows = [e[t : t + 1, :] for t in range(4)] + [taps[k : k + 1, :] for k in range(4)]
    rows += [ntab[t : t + 1, :] for t in range(4)] + [gin[...], gmid[...]]
    row = lax.broadcasted_iota(jnp.int32, (LANES, dim), 0)
    table = jnp.zeros((LANES, dim), F32)
    for i, r in enumerate(rows):
        table = jnp.where(row == i, r, table)
    cols[...] = table.T
    coefs = jnp.zeros((LANES, dim), F32)
    for k in range(4):
        for t in range(4):
            value = taps[k : k + 1, :] * ntab[t : t + 1, :]
            high = value.astype(BF16).astype(F32)
            at = 4 * k + t
            coefs = jnp.where((row == at) | (row == 32 + at), high, coefs)
            coefs = jnp.where(row == 16 + at, value - high, coefs)
    acat[...] = coefs.T[:, 0:48].astype(BF16)


def over_near_kernel(got, msg, *, rows, freqs):
    near, far, half, dim = got.shape
    own = msg.shape[1]
    peers = msg.shape[0] // far
    free = rows + freqs
    lane = lax.broadcasted_iota(jnp.int32, (1, dim), 1)
    row = lax.broadcasted_iota(jnp.int32, (own, LANES), 0)
    spare = lax.broadcasted_iota(jnp.int32, (own, LANES), 1) >= free
    for y in range(far):
        total = got[0, y].astype(F32)
        for i in range(1, near):
            total += got[i, y].astype(F32)
        bottom = pltpu.roll(total, dim // 2, 1)
        at = rows + freqs - half
        high = pltpu.roll(bottom, dim // 2, 1)[at + 1 : at + 2, :]
        small = jnp.where(lane < dim // 2, bottom[at : at + 1, :], high)
        both = jnp.concatenate([total, bottom], axis=0)
        both = jnp.concatenate([both, jnp.zeros((LANES - 2 * half, dim), F32)], axis=0)
        turned = both[:, 0 : 2 * LANES].T
        wide = jnp.broadcast_to(small, (8, dim))
        lines = jnp.zeros((own, LANES), F32)
        for m in range(dim // own):
            moved = pltpu.roll(wide, (free - own * m) % dim, 1)[0:1, 0:LANES]
            lines = jnp.where(row == m, moved, lines)
        for p in range(peers):
            part = turned[p * own : (p + 1) * own, :]
            msg[y * peers + p] = jnp.where(spare, lines, part).astype(BF16)


def over_far_kernel(got, g_mlp, msg, *, freqs):
    total = got[0].astype(F32)
    for i in range(1, got.shape[0]):
        total += got[i].astype(F32)
    own, rows = g_mlp.shape
    g_mlp[...] = total[0:own, 0:rows]
    lane = lax.broadcasted_iota(jnp.int32, (own, LANES), 1)
    part = jnp.where(lane < freqs, pltpu.roll(total[0:own, :], LANES - rows, 1), 0.0)
    first = part[0:8, :]
    for j in range(1, own // 8):
        first += pltpu.roll(part[8 * j : 8 * j + 8, :], freqs * j, 1)
    free = rows + freqs
    dim = 3 * LANES
    lane = lax.broadcasted_iota(jnp.int32, (8, LANES), 1)
    small = jnp.zeros((8, dim), F32)
    for m in range(dim // own):
        line = jnp.broadcast_to(total[m : m + 1, :], (8, LANES))
        line = jnp.where((lane >= free) & (lane < free + own), line, 0.0)
        wide = jnp.concatenate([line, jnp.zeros((8, dim - LANES), F32)], axis=1)
        shift = (own * m - free) % dim
        small += wide if shift == 0 else pltpu.roll(wide, shift, 1)
    row = lax.broadcasted_iota(jnp.int32, (8, LANES), 0)
    lines = jnp.zeros((8, LANES), F32)
    for j in range(dim // LANES):
        lines = jnp.where(row == j, small[:, j * LANES : (j + 1) * LANES], lines)
    whole = jnp.concatenate([first, lines], axis=0).astype(BF16)
    for i in range(msg.shape[0]):
        msg[i] = whole


def final_kernel(got, g_filter, g_emb, g_gin, g_conv, g_mid):
    own, group = g_filter.shape
    dim = g_emb.shape[1]
    peers = got.shape[0]
    freqs = group // peers
    per = LANES // freqs
    lane = lax.broadcasted_iota(jnp.int32, (8, LANES), 1)
    lines = []
    for c in range(group // LANES):
        tiles = [jnp.zeros((8, LANES), F32) for _ in range(own // 8)]
        for q in range(per):
            x = got[c * per + q].astype(F32)
            if len(lines) < 10:
                lines.append([x[8 + j : 9 + j, :] for j in range(dim // LANES)])
            mine = (lane >= q * freqs) & (lane < (q + 1) * freqs)
            for j in range(own // 8):
                shift = (q - j) * freqs % LANES
                y = x[0:8, :] if shift == 0 else pltpu.roll(x[0:8, :], shift, 1)
                tiles[j] = jnp.where(mine, y, tiles[j])
        for j in range(own // 8):
            g_filter[8 * j : 8 * j + 8, c * LANES : (c + 1) * LANES] = tiles[j]
    for j in range(dim // LANES):
        lanes = slice(j * LANES, (j + 1) * LANES)
        for t in range(4):
            g_emb[t : t + 1, lanes] = lines[t][j]
            g_conv[t : t + 1, lanes] = lines[5 + t][j]
    g_gin[...] = jnp.concatenate(lines[4], axis=1)[0, :]
    g_mid[...] = jnp.concatenate(lines[9], axis=1)[0, :]


def split_to(x, axis):
    return lax.all_to_all(x, axis, 0, 0, tiled=True)


def swapped(x, axis, distance):
    return lax.ppermute(x, axis, [(i, i ^ distance) for i in range(lax.axis_size(axis))])


def added(a, b):
    return (a.astype(F32) + b.astype(F32)).astype(BF16)


def kernel_call(body, outs, ins, scratch=(), smem=0, flops=0, name=None):
    vmem = pl.BlockSpec(memory_space=pltpu.VMEM)
    moved = sum(x.size * x.dtype.itemsize for x in ins)
    moved += sum(int(np.prod(o.shape)) * o.dtype.itemsize for o in outs)
    return pl.pallas_call(
        body,
        out_shape=tuple(outs),
        in_specs=[pl.BlockSpec(memory_space=pltpu.SMEM)] * smem + [vmem] * (len(ins) - smem),
        out_specs=tuple([vmem] * len(outs)),
        scratch_shapes=list(scratch),
        compiler_params=pltpu.CompilerParams(vmem_limit_bytes=48 * 1024 * 1024),
        cost_estimate=pl.CostEstimate(flops=flops, bytes_accessed=moved, transcendentals=0),
        name=name,
    )(*ins)


def on_device(tokens, embedding, gain_in, conv_taps, long_filter, gain_mid, mlp_weights, cotangent):
    span = tokens.shape[1]
    dim = embedding.shape[1]
    hidden = mlp_weights.shape[0] // 3
    own_ch, group = long_filter.shape
    shards = lax.axis_size(SEQ)
    dps = lax.axis_size(DP)
    near, far = lax.axis_size(NEAR), lax.axis_size("dp_y")
    per_block = group // span
    groups = shards // per_block
    chunks = group // LANES
    half = chunks // 2
    place = lax.axis_index(SEQ)
    core = lax.axis_index("dp_c")
    shape = jax.ShapeDtypeStruct

    vec = jnp.stack([place, core, place // per_block])
    where = vec.astype(jnp.int32)
    (msg,) = kernel_call(
        gather_kernel,
        [shape((shards, half * own_ch + 16, LANES), BF16)],
        [where, long_filter, tokens],
        smem=1,
        name="gather",
    )
    gath = split_to(msg, SEQ)

    table = dct_table(group)
    qt = jnp.asarray(np.ascontiguousarray(table.T))
    inner = (place % per_block) * span
    qown = lax.dynamic_slice_in_dim(jnp.asarray(table), inner, span, 1)
    qtown = lax.dynamic_slice_in_dim(qt, inner, span, 0)
    wt = mlp_weights.T
    cols, acat = kernel_call(
        prep_kernel,
        [shape((dim, LANES), F32), shape((dim, 48), BF16)],
        [embedding, conv_taps.T, gain_in[None], gain_mid[None]],
        name="prep",
    )

    bo, ba = kernel_call(
        back_kernel,
        [shape((dim, 2 * span), BF16), shape((hidden, 2 * span), BF16)],
        [cotangent[0], mlp_weights],
        flops=4 * hidden * dim * span,
        name="back",
    )
    gath, bo, ba, wt, qown, qtown, acat, cols = lax.optimization_barrier(
        (gath, bo, ba, wt, qown, qtown, acat, cols)
    )
    gath_other = swapped(gath, "dp_c", 1)
    (ohq,) = kernel_call(
        partial(dct_kernel, half_rows=half * own_ch, per_block=per_block),
        [shape((2, groups, 48, group), BF16)],
        [gath, qt],
        flops=2 * 128 * group * group,
        name="bases",
    )
    own_rows = 3 * hidden // dps
    freqs = group // dps
    all_rows = own_rows + freqs + 8
    all_rows += -all_rows % 16
    half_rows = all_rows // 2
    act, level, keep, send = kernel_call(
        mid_kernel,
        [
            shape((hidden, 2 * span), BF16),
            shape((dim, 2 * span), F32),
            shape((near, far, half_rows, dim), BF16),
            shape((near, far, half_rows, dim), BF16),
        ],
        [where, gath, gath_other, tokens, cols, acat, mlp_weights, wt, qown, qtown, ohq, bo, ba],
        scratch=[
            pltpu.VMEM((chunks, dim, LANES), F32),
            pltpu.VMEM((dim, group), BF16),
            pltpu.VMEM((dim, group), BF16),
            pltpu.VMEM((dim, span), BF16),
            pltpu.VMEM((dim, 2 * span), BF16),
            pltpu.VMEM((2 * hidden, 2 * span), BF16),
            pltpu.VMEM((3 * hidden, dim), F32),
            pltpu.VMEM((dim, group), F32),
            pltpu.VMEM((dps, all_rows - own_rows, dim), F32),
        ],
        smem=1,
        flops=28 * hidden * dim * span,
        name="mid",
    )
    (layer,) = kernel_call(
        out_kernel, [shape((2 * dim, span), BF16)], [level, act, wt], flops=4 * hidden * dim * span, name="out"
    )
    block = split_to(added(keep, swapped(send, "dp_c", 1)), NEAR)
    (msg,) = kernel_call(
        partial(over_near_kernel, rows=own_rows, freqs=freqs),
        [shape((far * shards // 2, own_ch, LANES), BF16)],
        [block],
        name="over_near",
    )
    grad_mlp, msg = kernel_call(
        partial(over_far_kernel, freqs=freqs),
        [shape((own_ch, own_rows), F32), shape((dps, 16, LANES), BF16)],
        [split_to(msg, FAR)],
        name="over_far",
    )
    grad_filter, grad_embedding, grad_gain_in, grad_conv, grad_gain_mid = kernel_call(
        final_kernel,
        [
            shape((own_ch, group), F32),
            shape((4, dim), F32),
            shape((dim,), F32),
            shape((4, dim), F32),
            shape((dim,), F32),
        ],
        [split_to(msg, DP)],
        name="final",
    )
    return (
        layer[None],
        grad_embedding,
        grad_gain_in,
        grad_conv.T,
        grad_filter,
        grad_gain_mid,
        grad_mlp.T,
    )


def solution(mesh):
    dps, seqs = mesh.devices.shape
    torus = Mesh(mesh.devices.reshape(dps // 8, 2, 2, 2, seqs // 4, 2, 2), DP + SEQ)
    return jax.shard_map(
        on_device,
        mesh=torus,
        in_specs=(P(DP, SEQ), P(), P(), P(), P(SEQ, None), P(), P(), P(DP, None, SEQ)),
        out_specs=(P(DP, None, SEQ), P(), P(), P(), P(SEQ, None), P(), P(DP, SEQ)),
        check_vma=False,
    )
```
